128 devices in a mesh: row: 8 (over x_hi, z), col: 8 (over y, core), fsdp: 2 (over x_lo).
Axes of the slice: x: 4 (x_hi: 2, x_lo: 2; x = x_hi * 2 + x_lo), y: 4, z: 4, core: 2. Of those that a mesh axis runs over, the one named last changes fastest.
Arguments:
- delta_one: float32 [8, 8, 1024, 2048], P('row', 'col', 'fsdp'), may hold values from -6 to 6
- delta_two: float32 [8, 8, 1024, 2048], P('row', 'col', 'fsdp'), may hold values from -6 to 6
- params_one: float32 [8, 1024, 2048], P('row', 'fsdp', 'col'), may hold values from -6 to 6
- moment_one: float32 [8, 1024, 2048], P('row', 'fsdp', 'col'), may hold values from -6 to 6
- params_two: float32 [8, 1024, 2048], P('col', 'fsdp', 'row'), may hold values from -6 to 6
- moment_two: float32 [8, 1024, 2048], P('col', 'fsdp', 'row'), may hold values from -6 to 6
Outputs:
- new_params_one: float32 [8, 1024, 2048], P('row', 'fsdp', 'col')
- new_moment_one: float32 [8, 1024, 2048], P('row', 'fsdp', 'col')
- copy_one: bfloat16 [8, 1024, 2048], P('row', 'fsdp')
- new_params_two: float32 [8, 1024, 2048], P('col', 'fsdp', 'row')
- new_moment_two: float32 [8, 1024, 2048], P('col', 'fsdp', 'row')
- copy_two: bfloat16 [8, 1024, 2048], P('col', 'fsdp')
The draws below stay inside these ranges and needn't reach their ends.
All inputs are finite; a program needn't handle non-finite values.
Results may differ from the reference program's by a relative error of at most 0.001.
Values may be sent and summed in bfloat16 or wider, within the bound.
A program may use at most 128 MiB of HBM per device.

```python
import jax
import jax.numpy as jnp

D = 1024
FF_WIN = 2048
N_ROW = 8
N_COL = 8


def raised(result, stream_key, source, target, shards_of, factor):
    owner, partner = [(jnp.arange(result.shape[dim]) // (result.shape[dim] // shards_of)).reshape([-1 if axis == dim else 1 for axis in range(result.ndim)]) for dim in (source, target)]
    chosen = jax.random.permutation(stream_key, shards_of)[partner]
    strong = (owner == chosen) | (owner == (partner + shards_of // 2) % shards_of)
    return jnp.where(strong, factor * result, result)


def levels(stream_key, shape, cuts, smallest, largest):
    loudness, own = 1.0, jax.random.fold_in(stream_key, 6)
    for axis_at, shards_of in cuts:
        draws = jnp.exp(jax.random.uniform(jax.random.fold_in(own, axis_at), (shards_of,), jnp.float32, smallest / len(cuts), largest / len(cuts)))
        loudness = loudness * jnp.repeat(draws, shape[axis_at] // shards_of).reshape([-1 if axis == axis_at else 1 for axis in range(len(shape))])
    return loudness


def bell_draw(rng, extent, width, limit, shards=(), dtype=jnp.bfloat16):
    result = jax.random.normal(rng, extent, jnp.float32) * width
    if len(shards) > 0:
        result = levels(rng, extent, shards, -0.22, 0.18) * result
    return jnp.clip(result, min=-limit, max=limit).astype(dtype)


def noise_with(stream_key, shape, scale, most, cuts, heavy, dtype=jnp.bfloat16):
    array = scale * jax.random.normal(stream_key, shape, jnp.float32)
    if cuts:
        array = array * levels(stream_key, shape, cuts, -0.22, 0.18)
    return jnp.clip(raised(array, jax.random.fold_in(stream_key, 3), *heavy), -most, most).astype(dtype)


def setup_inputs(seed: int = 0) -> dict:
    seeds = jax.random.split(jax.random.key(seed), 7)
    delta_one = noise_with(seeds[0], (N_ROW, N_COL, D, FF_WIN), 1.0, 6.0, ((0, 8), (1, 8), (2, 2)), (1, 3, 8, 2.0), jnp.float32)
    delta_two = noise_with(seeds[1], (N_ROW, N_COL, D, FF_WIN), 1.0, 6.0, ((0, 8), (1, 8), (2, 2)), (0, 3, 8, 2.0), jnp.float32)
    params_one = bell_draw(seeds[2], (N_ROW, D, FF_WIN), 1.0, 6.0, ((0, 8), (1, 2), (2, 8)), jnp.float32)
    moment_one = bell_draw(seeds[3], (N_ROW, D, FF_WIN), 1.0, 6.0, ((0, 8), (1, 2), (2, 8)), jnp.float32)
    params_two = bell_draw(seeds[4], (N_COL, D, FF_WIN), 1.0, 6.0, ((0, 8), (1, 2), (2, 8)), jnp.float32)
    moment_two = bell_draw(seeds[5], (N_COL, D, FF_WIN), 1.0, 6.0, ((0, 8), (1, 2), (2, 8)), jnp.float32)
    return dict(delta_one=delta_one, delta_two=delta_two, params_one=params_one, moment_one=moment_one, params_two=params_two, moment_two=moment_two)


def nesterov(grad, params, moment):
    moment_next = 0.9 * moment + grad
    params_next = params - 0.7 * (grad + 0.9 * moment_next)
    return params_next, moment_next, params_next.astype(jnp.bfloat16)


def reference(delta_one, delta_two, params_one, moment_one, params_two, moment_two):
    grad_one = jnp.sum(delta_one, axis=1) / N_COL
    grad_two = jnp.sum(delta_two, axis=0) / N_ROW
    first_params, first_moment, first_copy = nesterov(grad_one, params_one, moment_one)
    second_params, second_moment, second_copy = nesterov(grad_two, params_two, moment_two)
    return first_params, first_moment, first_copy, second_params, second_moment, second_copy
```

```python
import jax
import jax.numpy as jnp
from jax import lax
from jax.experimental import pallas as pl
from jax.experimental.pallas import tpu as pltpu
from jax.sharding import PartitionSpec as P

MESH = pl.DeviceIdType.MESH
ROWS, WIDTH = 512, 256
STEP = 16
PIECES_TWO = ((0, 0, 96), (1, 96, 96), (2, 192, 80), (0, 272, 80), (1, 352, 80), (2, 432, 80))
PIECES_ONE = ((0, 0, 128), (1, 128, 128), (0, 256, 128), (1, 384, 128))
N_COPIES = 14 * (len(PIECES_TWO) + len(PIECES_ONE))


def code(x, power):
    t = x * (2.0**power)
    t2 = t * t
    return ((t2 * t2) * t2 * (t * jnp.abs(t))).astype(jnp.bfloat16)


def decode(y, power):
    y = y.astype(jnp.float32)
    quarter = lax.rsqrt(lax.rsqrt(jnp.maximum(jnp.abs(y), 2.0**-126)))
    sign = jnp.where(y < 0, -(2.0**-power), 2.0**-power)
    return quarter * lax.rsqrt(quarter) * sign


def kernel(
    d1, d2, p1, m1, p2, m2,
    np1, nm1, c1, np2, nm2, c2,
    d1v, d2v, pm, pmo, cv1, cv2,
    s2a, s2b, s2c, r2a, r2b, r2c,
    s1b, s1c, r1a, r1b, r1c,
    send_sem, recv_sem, load_sem, store_sem,
):
    row, col, fsdp = lax.axis_index("row"), lax.axis_index("col"), lax.axis_index("fsdp")
    xh, z = row // 4, row % 4
    y, core = col // 2, col % 2

    def flip4(v, mask):
        if mask == 0:
            return v
        if mask == 1:
            return v + 1 - 2 * (v % 2)
        if mask == 3:
            return 3 - v
        return 2 - v + 2 * (v % 2)

    def row_of(mask):
        high = 1 - xh if mask & 4 else xh
        return high * 4 + flip4(z, mask & 3)

    def col_of(mask):
        low = 1 - core if mask & 1 else core
        return flip4(y, mask >> 1) * 2 + low

    def device_two(mask):
        return (row_of(mask), col, fsdp)

    def device_one(mask):
        return (row, col_of(mask), fsdp)

    orders_two = ((1, 3, 4), (3, 4, 1), (4, 1, 3))
    orders_one = ((1, 2, 6), (1, 6, 2))

    def cols(index):
        return pl.ds(pl.multiple_of(index * WIDTH, WIDTH), WIDTH)

    n_sent = [0]
    sent = []

    def send(src, dst, device):
        i = n_sent[0]
        n_sent[0] += 1
        copy = pltpu.make_async_remote_copy(
            src_ref=src, dst_ref=dst, send_sem=send_sem.at[i], recv_sem=recv_sem.at[i],
            device_id=device, device_id_type=MESH,
        )
        copy.start()
        sent.append(copy)
        return copy

    loads, stores = [], []

    def load(src, dst):
        copy = pltpu.make_async_copy(src, dst, load_sem.at[len(loads)])
        copy.start()
        loads.append(copy)
        return copy

    def store(src, dst):
        copy = pltpu.make_async_copy(src, dst, store_sem.at[len(stores)])
        copy.start()
        stores.append(copy)
        return copy

    loaded_two, loaded_one = {}, {}
    for k, (o, r0, n) in enumerate(PIECES_TWO):
        loaded_two[k] = load(d2.at[pl.ds(r0, n)], d2v.at[pl.ds(r0, n)])
    for k, (o, r0, n) in enumerate(PIECES_ONE):
        loaded_one[k] = load(d1.at[pl.ds(r0, n)], d1v.at[pl.ds(r0, n)])
    loaded_pm = [load(ref, pm.at[i]) for i, ref in enumerate((p1, m1, p2, m2))]

    barrier = pltpu.get_barrier_semaphore()
    for mask in (1, 3, 4):
        pl.semaphore_signal(barrier, inc=1, device_id=device_two(mask), device_id_type=MESH)
    for mask in (1, 2, 6):
        pl.semaphore_signal(barrier, inc=1, device_id=device_one(mask), device_id_type=MESH)
    pl.semaphore_wait(barrier, 6)

    def over(r0, n, body):
        def step(i, carry):
            body(pl.ds(pl.multiple_of(r0 + i * STEP, STEP), STEP))
            return carry

        lax.fori_loop(0, n // STEP, step, 0)

    def block_mask(order, e):
        mask = 0
        for bit, m in zip((4, 2, 1), order):
            if e & bit:
                mask ^= m
        return mask

    class Level:
        def __init__(self, pieces, orders, index_of, device, dv, cv, loaded, param, out, copy_out):
            self.pieces, self.orders, self.index_of, self.device = pieces, orders, index_of, device
            self.dv, self.cv, self.loaded = dv, cv, loaded
            self.param, self.out, self.copy_out = param, out, copy_out
            self.got = {}

        def at(self, k):
            o, r0, n = self.pieces[k]
            return self.orders[o], r0, n, pl.ds(r0, n)

        def cols(self, order, e):
            return cols(self.index_of(block_mask(order, e)))

        def give(self, k, e, stage):
            order, r0, n, rs = self.at(k)
            part = self.cv.at[rs, self.cols(order, e)]
            bit = (4, 2, 1)[stage]
            self.got[k, e ^ bit] = send(part, part, self.device(order[stage]))

        def finish(self, k, grad_of):
            order, r0, n, rs = self.at(k)
            mine = self.cols(order, 0)
            i = self.param

            def body(s):
                grad = grad_of(s) * 0.125
                moment = 0.9 * pm[i + 1, s] + grad
                params = pm[i, s] - 0.7 * (grad + 0.9 * moment)
                pmo[i + 1, s] = moment
                pmo[i, s] = params
                self.cv[s, mine] = params.astype(jnp.bfloat16)

            over(r0, n, body)
            self.give(k, 0, 2)
            self.give(k, 0, 1)
            self.give(k, 0, 0)
            store(pmo.at[i, rs], self.out[0].at[rs])
            store(pmo.at[i + 1, rs], self.out[1].at[rs])

        def gather_a(self, k):
            self.got[k, 1].wait_recv()
            self.give(k, 1, 1)
            self.give(k, 1, 0)

        def gather_b(self, k):
            self.got[k, 2].wait_recv()
            self.give(k, 2, 0)
            self.got[k, 3].wait_recv()
            self.give(k, 3, 0)

        def gather_c(self, k):
            order, r0, n, rs = self.at(k)
            for e in (4, 5, 6, 7):
                self.got[k, e].wait_recv()
            store(self.cv.at[rs], self.copy_out.at[rs])

    two = Level(PIECES_TWO, orders_two, row_of, device_two, d2v, cv2, loaded_two, 2, (np2, nm2), c2)
    one = Level(PIECES_ONE, orders_one, col_of, device_one, d1v, cv1, loaded_one, 0, (np1, nm1), c1)
    red = {}

    def two_a(k):
        order, r0, n, rs = two.at(k)
        loaded_two[k].wait()
        for q_pair in ((3, 2), (1, 0)):
            places = [(q, two.cols(order, 4 + q)) for q in q_pair]

            def body(s):
                for q, c in places:
                    s2a[q, s] = code(d2v[s, c], 13)

            over(r0, n, body)
            for q in q_pair:
                red["2a", k, q] = send(s2a.at[q, rs], r2a.at[q, rs], two.device(order[0]))

    def two_b(k):
        order, r0, n, rs = two.at(k)
        red["2a", k, 3].wait_recv()
        red["2a", k, 2].wait_recv()
        places = [(q, two.cols(order, 2 + q)) for q in (1, 0)]

        def body(s):
            for q, c in places:
                s2b[q, s] = code(d2v[s, c] + decode(r2a[2 + q, s], 13), 12)

        over(r0, n, body)
        for q in (1, 0):
            red["2b", k, q] = send(s2b.at[q, rs], r2b.at[q, rs], two.device(order[1]))

    def two_c(k):
        order, r0, n, rs = two.at(k)
        red["2a", k, 1].wait_recv()
        red["2b", k, 1].wait_recv()
        c = two.cols(order, 1)

        def body(s):
            s2c[s] = code(d2v[s, c] + decode(r2a[1, s], 13) + decode(r2b[1, s], 12), 11)

        over(r0, n, body)
        red["2c", k] = send(s2c.at[rs], r2c.at[rs], two.device(order[2]))

    def two_d(k):
        order, r0, n, rs = two.at(k)
        red["2a", k, 0].wait_recv()
        red["2b", k, 0].wait_recv()
        red["2c", k].wait_recv()
        c = two.cols(order, 0)
        two.finish(k, lambda s: d2v[s, c] + decode(r2a[0, s], 13) + decode(r2b[0, s], 12) + decode(r2c[s], 11))

    def one_a(k):
        order, r0, n, rs = one.at(k)
        for q in (3, 2, 1, 0):
            red["1a", k, q] = send(d1.at[rs, one.cols(order, 4 + q)], r1a.at[q, rs], one.device(order[0]))

    def one_b(k):
        order, r0, n, rs = one.at(k)
        loaded_one[k].wait()
        red["1a", k, 3].wait_recv()
        red["1a", k, 2].wait_recv()
        places = [(q, one.cols(order, 2 + q)) for q in (1, 0)]

        def body(s):
            for q, c in places:
                s1b[q, s] = d1v[s, c] + r1a[2 + q, s]

        over(r0, n, body)
        for q in (1, 0):
            red["1b", k, q] = send(s1b.at[q, rs], r1b.at[q, rs], one.device(order[1]))

    def one_c(k):
        order, r0, n, rs = one.at(k)
        red["1a", k, 1].wait_recv()
        red["1b", k, 1].wait_recv()
        c = one.cols(order, 1)

        def body(s):
            s1c[s] = d1v[s, c] + r1a[1, s] + r1b[1, s]

        over(r0, n, body)
        red["1c", k] = send(s1c.at[rs], r1c.at[rs], one.device(order[2]))

    def one_d(k):
        order, r0, n, rs = one.at(k)
        red["1a", k, 0].wait_recv()
        red["1b", k, 0].wait_recv()
        red["1c", k].wait_recv()
        c = one.cols(order, 0)
        one.finish(k, lambda s: d1v[s, c] + r1a[0, s] + r1b[0, s] + r1c[s])

    for k in range(4):
        one_a(k)
    for k in range(3):
        two_a(k)
    for k in range(2):
        one_b(k)
    for k in range(3, 6):
        two_a(k)
    for k in range(2, 4):
        one_b(k)
    for k in range(3):
        two_b(k)
    for k in range(3, 6):
        two_b(k)
    for k in range(3):
        two_c(k)
    for k in range(2):
        one_c(k)
    for k in range(3, 6):
        two_c(k)
    for copy in loaded_pm:
        copy.wait()
    for k in range(3):
        two_d(k)
    for k in range(2, 4):
        one_c(k)
    for k in range(3, 6):
        two_d(k)
    for k in range(3):
        two.gather_a(k)
    for k in range(2):
        one_d(k)
    for k in range(3, 6):
        two.gather_a(k)
    for k in range(3):
        two.gather_b(k)
    for k in range(2, 4):
        one_d(k)
    for k in range(2):
        one.gather_a(k)
    for k in range(3, 6):
        two.gather_b(k)
    for k in range(2):
        one.gather_b(k)
    for k in range(2, 4):
        one.gather_a(k)
    for k in range(3):
        two.gather_c(k)
    for k in range(2, 4):
        one.gather_b(k)
    for k in range(2):
        one.gather_c(k)
    for k in range(3, 6):
        two.gather_c(k)
    for k in range(2, 4):
        one.gather_c(k)
    for copy in sent:
        copy.wait_send()
    for copy in stores:
        copy.wait()
    assert n_sent[0] == N_COPIES


def body(delta_one, delta_two, params_one, moment_one, params_two, moment_two):
    hbm = pl.BlockSpec(memory_space=pl.ANY)
    small = jax.ShapeDtypeStruct((ROWS, WIDTH), jnp.float32)
    wide = jax.ShapeDtypeStruct((ROWS, 8 * WIDTH), jnp.bfloat16)
    f32, bf16 = jnp.float32, jnp.bfloat16
    n_local = len(PIECES_TWO) + len(PIECES_ONE)
    outs = pl.pallas_call(
        kernel,
        out_shape=(small, small, wide, small, small, wide),
        in_specs=[hbm] * 6,
        out_specs=[hbm] * 6,
        scratch_shapes=[
            pltpu.VMEM((ROWS, 8 * WIDTH), f32),
            pltpu.VMEM((ROWS, 8 * WIDTH), f32),
            pltpu.VMEM((4, ROWS, WIDTH), f32),
            pltpu.VMEM((4, ROWS, WIDTH), f32),
            pltpu.VMEM((ROWS, 8 * WIDTH), bf16),
            pltpu.VMEM((ROWS, 8 * WIDTH), bf16),
            pltpu.VMEM((4, ROWS, WIDTH), bf16),
            pltpu.VMEM((2, ROWS, WIDTH), bf16),
            pltpu.VMEM((ROWS, WIDTH), bf16),
            pltpu.VMEM((4, ROWS, WIDTH), bf16),
            pltpu.VMEM((2, ROWS, WIDTH), bf16),
            pltpu.VMEM((ROWS, WIDTH), bf16),
            pltpu.VMEM((2, ROWS, WIDTH), f32),
            pltpu.VMEM((ROWS, WIDTH), f32),
            pltpu.VMEM((4, ROWS, WIDTH), f32),
            pltpu.VMEM((2, ROWS, WIDTH), f32),
            pltpu.VMEM((ROWS, WIDTH), f32),
            pltpu.SemaphoreType.DMA((N_COPIES,)),
            pltpu.SemaphoreType.DMA((N_COPIES,)),
            pltpu.SemaphoreType.DMA((n_local + 4,)),
            pltpu.SemaphoreType.DMA((3 * n_local,)),
        ],
        compiler_params=pltpu.CompilerParams(
            collective_id=0, has_side_effects=True, vmem_limit_bytes=48 * 1024 * 1024
        ),
        name="outer_step",
    )(delta_one[0, 0], delta_two[0, 0], params_one[0], moment_one[0], params_two[0], moment_two[0])
    return tuple(out[None] for out in outs)


def solution(mesh):
    placed = (
        P("row", "col", "fsdp", None),
        P("row", "col", "fsdp", None),
        P("row", "fsdp", "col"),
        P("row", "fsdp", "col"),
        P("col", "fsdp", "row"),
        P("col", "fsdp", "row"),
    )
    return jax.shard_map(
        body,
        mesh=mesh,
        in_specs=placed,
        out_specs=(
            P("row", "fsdp", "col"),
            P("row", "fsdp", "col"),
            P("row", "fsdp", None),
            P("col", "fsdp", "row"),
            P("col", "fsdp", "row"),
            P("col", "fsdp", None),
        ),
        check_vma=False,
    )
```

```python
import jax
import jax.numpy as jnp
from jax import lax
from jax.experimental import pallas as pl
from jax.experimental.pallas import tpu as pltpu
from jax.sharding import PartitionSpec as P

MESH = pl.DeviceIdType.MESH
ROWS, WIDTH = 512, 256
STEP = 16
PIECES_TWO = ((0, 0, 96), (1, 96, 96), (2, 192, 80), (0, 272, 80), (1, 352, 80), (2, 432, 80))
PIECES_ONE = ((0, 0, 128), (1, 128, 128), (0, 256, 128), (1, 384, 128))
PLAN = (
    (2, "a", 0), (2, "a", 1), (2, "a", 2), (2, "a", 3), (2, "a", 4), (2, "a", 5),
    (1, "a", 0), (1, "a", 1), (1, "a", 2), (1, "a", 3), (2, "b", 0), (2, "b", 1),
    (2, "b", 2), (1, "b", 0), (1, "b", 1), (1, "b", 2), (2, "b", 3), (1, "b", 3),
    (1, "c", 0), (2, "b", 4), (2, "b", 5), (1, "c", 1), (2, "c", 2), (2, "c", 1),
    (2, "c", 0), (1, "c", 2), (2, "c", 5), (1, "c", 3), (2, "c", 4), (2, "c", 3),
    (1, "d", 1), (2, "d", 1), (2, "d", 2), (2, "d", 0), (1, "d", 0), (2, "d", 5),
    (2, "d", 3), (2, "d", 4), (1, "d", 2), (1, "d", 3), (2, "e", 1), (1, "e", 1),
    (2, "e", 2), (1, "e", 0), (2, "e", 0), (2, "e", 5), (1, "e", 2), (2, "e", 3),
    (1, "e", 3), (2, "e", 4), (2, "f", 2), (2, "f", 1), (1, "f", 0), (1, "f", 1),
    (2, "f", 0), (1, "f", 2), (1, "g", 0), (2, "f", 5), (1, "g", 1), (2, "f", 3),
    (1, "f", 3), (2, "f", 4), (1, "g", 2), (1, "g", 3), (2, "g", 2), (2, "g", 1),
    (2, "g", 0), (2, "g", 5), (2, "g", 4), (2, "g", 3),
)
N_COPIES = 14 * (len(PIECES_TWO) + len(PIECES_ONE))


def code(x, power):
    t = x * (2.0**power)
    t2 = t * t
    return ((t2 * t2) * t2 * (t * jnp.abs(t))).astype(jnp.bfloat16)


def decode(y, power):
    y = y.astype(jnp.float32)
    quarter = lax.rsqrt(lax.rsqrt(jnp.maximum(jnp.abs(y), 2.0**-126)))
    sign = jnp.where(y < 0, -(2.0**-power), 2.0**-power)
    return quarter * lax.rsqrt(quarter) * sign


def kernel(
    d1, d2, p1, m1, p2, m2,
    np1, nm1, cv1, np2, nm2, cv2,
    d1v, d2v, pm,
    s2a, s2b, s2c, r2a, r2b, r2c,
    s1b, s1c, r1a, r1b, r1c,
    send_sem, recv_sem, load_sem,
):
    row, col, fsdp = lax.axis_index("row"), lax.axis_index("col"), lax.axis_index("fsdp")
    xh, z = row // 4, row % 4
    y, core = col // 2, col % 2

    def flip4(v, mask):
        if mask == 0:
            return v
        if mask == 1:
            return v + 1 - 2 * (v % 2)
        if mask == 3:
            return 3 - v
        return 2 - v + 2 * (v % 2)

    def row_of(mask):
        high = 1 - xh if mask & 4 else xh
        return high * 4 + flip4(z, mask & 3)

    def col_of(mask):
        low = 1 - core if mask & 1 else core
        return flip4(y, mask >> 1) * 2 + low

    def device_two(mask):
        return (row_of(mask), col, fsdp)

    def device_one(mask):
        return (row, col_of(mask), fsdp)

    orders_two = ((1, 3, 4), (3, 4, 1), (4, 1, 3))
    orders_one = ((1, 2, 6), (1, 6, 2))

    def cols(index):
        return pl.ds(pl.multiple_of(index * WIDTH, WIDTH), WIDTH)

    barrier = pltpu.get_barrier_semaphore()
    for mask in (1, 3, 4):
        pl.semaphore_signal(barrier, inc=1, device_id=device_two(mask), device_id_type=MESH)
    for mask in (1, 2, 6):
        pl.semaphore_signal(barrier, inc=1, device_id=device_one(mask), device_id_type=MESH)

    n_sent = [0]
    sent = []

    def send(src, dst, device):
        i = n_sent[0]
        n_sent[0] += 1
        if i == 0:
            pl.semaphore_wait(barrier, 6)
        copy = pltpu.make_async_remote_copy(
            src_ref=src, dst_ref=dst, send_sem=send_sem.at[i], recv_sem=recv_sem.at[i],
            device_id=device, device_id_type=MESH,
        )
        copy.start()
        sent.append(copy)
        return copy

    loads = []

    def load(src, dst):
        copy = pltpu.make_async_copy(src, dst, load_sem.at[len(loads)])
        copy.start()
        loads.append(copy)
        return copy

    loaded_two, loaded_one = {}, {}
    for k in range(max(len(PIECES_TWO), len(PIECES_ONE))):
        for pieces, loaded, hbm, vmem in (
            (PIECES_TWO, loaded_two, d2, d2v),
            (PIECES_ONE, loaded_one, d1, d1v),
        ):
            if k < len(pieces):
                rs = pl.ds(pieces[k][1], pieces[k][2])
                loaded[k] = load(hbm.at[rs], vmem.at[rs])
    loaded_pm = [load(ref, pm.at[i]) for i, ref in enumerate((p1, m1, p2, m2))]

    def over(r0, n, body):
        def step(i, carry):
            body(pl.ds(pl.multiple_of(r0 + i * STEP, STEP), STEP))
            return carry

        lax.fori_loop(0, n // STEP, step, 0)

    def block_mask(order, e):
        mask = 0
        for bit, m in zip((4, 2, 1), order):
            if e & bit:
                mask ^= m
        return mask

    class Level:
        def __init__(self, pieces, orders, index_of, device, dv, cv, loaded, param, out, sa, sb, sc, ra, rb, rc):
            self.pieces, self.orders, self.index_of, self.device = pieces, orders, index_of, device
            self.dv, self.cv, self.loaded = dv, cv, loaded
            self.param, self.out = param, out
            self.sa, self.sb, self.sc, self.ra, self.rb, self.rc = sa, sb, sc, ra, rb, rc
            self.got = {}

        def at(self, k):
            o, r0, n = self.pieces[k]
            return self.orders[o], r0, n, pl.ds(r0, n)

        def cols(self, order, e):
            return cols(self.index_of(block_mask(order, e)))

        def give(self, k, e, stage):
            order, r0, n, rs = self.at(k)
            part = self.cv.at[rs, self.cols(order, e)]
            bit = (4, 2, 1)[stage]
            self.got[k, "g", e ^ bit] = send(part, part, self.device(order[stage]))

        def ready(self, k):
            if k in self.loaded:
                self.loaded.pop(k).wait()

        def want(self, *keys):
            for key in keys:
                self.got.pop(key).wait_recv()

        def step_b(self, k):
            order, r0, n, rs = self.at(k)
            self.ready(k)
            self.want((k, "a", 3), (k, "a", 2))
            places = [(q, self.cols(order, 2 + q)) for q in (1, 0)]

            def body(s):
                for q, c in places:
                    self.sb[q, s] = code(self.dv[s, c] + self.first(self.ra[2 + q, s]), 12)

            over(r0, n, body)
            for q in (1, 0):
                self.got[k, "b", q] = send(self.sb.at[q, rs], self.rb.at[q, rs], self.device(order[1]))

        def step_c(self, k):
            order, r0, n, rs = self.at(k)
            self.want((k, "a", 1), (k, "b", 1))
            c = self.cols(order, 1)

            def body(s):
                total = self.dv[s, c] + self.first(self.ra[1, s]) + decode(self.rb[1, s], 12)
                self.sc[s] = code(total, 11)

            over(r0, n, body)
            self.got[k, "c", 0] = send(self.sc.at[rs], self.rc.at[rs], self.device(order[2]))

        def step_d(self, k):
            order, r0, n, rs = self.at(k)
            self.want((k, "a", 0), (k, "b", 0), (k, "c", 0))
            mine = self.cols(order, 0)
            i = self.param

            def body(s):
                total = self.dv[s, mine] + self.first(self.ra[0, s])
                grad = (total + decode(self.rb[0, s], 12) + decode(self.rc[s], 11)) * 0.125
                moment = 0.9 * pm[i + 1, s] + grad
                params = pm[i, s] - 0.7 * (grad + 0.9 * moment)
                self.out[1][s] = moment
                self.out[0][s] = params
                self.cv[s, mine] = params.astype(jnp.bfloat16)

            over(r0, n, body)
            self.give(k, 0, 2)
            self.give(k, 0, 1)
            self.give(k, 0, 0)

        def step_e(self, k):
            self.want((k, "g", 1))
            self.give(k, 1, 1)
            self.give(k, 1, 0)

        def step_f(self, k):
            self.want((k, "g", 2))
            self.give(k, 2, 0)
            self.want((k, "g", 3))
            self.give(k, 3, 0)

        def step_g(self, k):
            self.want(*((k, "g", e) for e in (4, 5, 6, 7)))

    class Two(Level):
        def first(self, x):
            return decode(x, 13)

        def step_a(self, k):
            order, r0, n, rs = self.at(k)
            self.ready(k)
            for pair in ((3, 2), (1, 0)):
                places = [(q, self.cols(order, 4 + q)) for q in pair]

                def body(s):
                    for q, c in places:
                        self.sa[q, s] = code(self.dv[s, c], 13)

                over(r0, n, body)
                for q in pair:
                    self.got[k, "a", q] = send(self.sa.at[q, rs], self.ra.at[q, rs], self.device(order[0]))

    class One(Level):
        def first(self, x):
            return x

        def step_a(self, k):
            order, r0, n, rs = self.at(k)
            for q in (3, 2, 1, 0):
                part = d1.at[rs, self.cols(order, 4 + q)]
                self.got[k, "a", q] = send(part, self.ra.at[q, rs], self.device(order[0]))

    two = Two(PIECES_TWO, orders_two, row_of, device_two, d2v, cv2, loaded_two, 2, (np2, nm2), s2a, s2b, s2c, r2a, r2b, r2c)
    one = One(PIECES_ONE, orders_one, col_of, device_one, d1v, cv1, loaded_one, 0, (np1, nm1), None, s1b, s1c, r1a, r1b, r1c)
    for level, step, k in PLAN:
        if step == "d" and loaded_pm:
            for copy in loaded_pm:
                copy.wait()
            loaded_pm.clear()
        getattr(two if level == 2 else one, "step_" + step)(k)
    for copy in sent:
        copy.wait_send()
    assert n_sent[0] == N_COPIES


def write_out(*refs):
    sems = refs[12]
    copies = [pltpu.make_async_copy(refs[i], refs[6 + i], sems.at[i]) for i in range(6)]
    for copy in copies:
        copy.start()
    for copy in copies:
        copy.wait()


def body(delta_one, delta_two, params_one, moment_one, params_two, moment_two):
    args = (delta_one[0, 0], delta_two[0, 0], params_one[0], moment_one[0], params_two[0], moment_two[0])
    hbm = pl.BlockSpec(memory_space=pltpu.HBM)
    vmem = pl.BlockSpec(memory_space=pltpu.VMEM)
    small = jax.ShapeDtypeStruct((ROWS, WIDTH), jnp.float32)
    wide = jax.ShapeDtypeStruct((ROWS, 8 * WIDTH), jnp.bfloat16)
    f32, bf16 = jnp.float32, jnp.bfloat16
    n_local = len(PIECES_TWO) + len(PIECES_ONE)
    outs = pl.pallas_call(
        kernel,
        out_shape=tuple(pltpu.VMEM(x.shape, x.dtype) for x in (small, small, wide, small, small, wide)),
        in_specs=[hbm] * 6,
        out_specs=[vmem] * 6,
        scratch_shapes=[
            pltpu.VMEM((ROWS, 8 * WIDTH), f32),
            pltpu.VMEM((ROWS, 8 * WIDTH), f32),
            pltpu.VMEM((4, ROWS, WIDTH), f32),
            pltpu.VMEM((4, ROWS, WIDTH), bf16),
            pltpu.VMEM((2, ROWS, WIDTH), bf16),
            pltpu.VMEM((ROWS, WIDTH), bf16),
            pltpu.VMEM((4, ROWS, WIDTH), bf16),
            pltpu.VMEM((2, ROWS, WIDTH), bf16),
            pltpu.VMEM((ROWS, WIDTH), bf16),
            pltpu.VMEM((2, ROWS, WIDTH), bf16),
            pltpu.VMEM((ROWS, WIDTH), bf16),
            pltpu.VMEM((4, ROWS, WIDTH), f32),
            pltpu.VMEM((2, ROWS, WIDTH), bf16),
            pltpu.VMEM((ROWS, WIDTH), bf16),
            pltpu.SemaphoreType.DMA((N_COPIES,)),
            pltpu.SemaphoreType.DMA((N_COPIES,)),
            pltpu.SemaphoreType.DMA((n_local + 4,)),
        ],
        compiler_params=pltpu.CompilerParams(
            collective_id=0, has_side_effects=True, vmem_limit_bytes=32 * 1024 * 1024
        ),
        name="outer_step",
    )(*(pltpu.with_memory_space_constraint(x, pltpu.HBM) for x in args))
    outs = pl.pallas_call(
        write_out,
        out_shape=(small, small, wide, small, small, wide),
        in_specs=[vmem] * 6,
        out_specs=[hbm] * 6,
        scratch_shapes=[pltpu.SemaphoreType.DMA((6,))],
        compiler_params=pltpu.CompilerParams(vmem_limit_bytes=1024 * 1024),
        name="write_out",
    )(*(pltpu.with_memory_space_constraint(x, pltpu.VMEM) for x in outs))
    return tuple(out[None] for out in outs)


def solution(mesh):
    placed = (
        P("row", "col", "fsdp", None),
        P("row", "col", "fsdp", None),
        P("row", "fsdp", "col"),
        P("row", "fsdp", "col"),
        P("col", "fsdp", "row"),
        P("col", "fsdp", "row"),
    )
    return jax.shard_map(
        body,
        mesh=mesh,
        in_specs=placed,
        out_specs=(
            P("row", "fsdp", "col"),
            P("row", "fsdp", "col"),
            P("row", "fsdp", None),
            P("col", "fsdp", "row"),
            P("col", "fsdp", "row"),
            P("col", "fsdp", None),
        ),
        check_vma=False,
    )
```

```python
import jax
import jax.numpy as jnp
from jax import lax
from jax.experimental import pallas as pl
from jax.experimental.pallas import tpu as pltpu
from jax.sharding import PartitionSpec as P

MESH = pl.DeviceIdType.MESH
ROWS, WIDTH = 512, 256
STEP = 16
PIECES_TWO = ((0, 0, 64), (1, 64, 64), (2, 128, 48), (0, 176, 80), (1, 256, 64), (2, 320, 64), (0, 384, 48), (1, 432, 48), (2, 480, 32))
PIECES_ONE = ((0, 0, 96), (1, 96, 96), (0, 192, 160), (1, 352, 160))
PLAN = (
    (2, "a3", 0), (1, "a3", 0), (2, "a3", 1), (2, "a21", 0), (2, "a21", 1), (2, "a3", 2),
    (2, "a21", 2), (1, "a3", 2), (2, "a0", 0), (2, "a3", 3), (2, "a0", 1), (1, "b1", 0),
    (1, "b1", 1), (2, "a3", 4), (2, "a3", 5), (1, "b0", 0), (2, "a0", 2), (1, "b0", 1),
    (2, "a3", 6), (2, "a3", 7), (2, "a3", 8), (2, "a21", 3), (2, "b1", 0), (2, "a21", 4),
    (2, "a21", 5), (2, "b1", 1), (2, "b1", 2), (1, "b1", 2), (1, "b1", 3), (2, "b0", 0),
    (1, "b0", 2), (2, "b0", 1), (2, "b0", 2), (1, "b0", 3), (1, "c", 0), (1, "c", 1),
    (2, "b1", 5), (2, "b1", 3), (2, "b1", 4), (2, "b1", 6), (2, "b1", 8), (2, "b1", 7),
    (2, "a0", 3), (2, "a0", 4), (2, "a0", 5), (2, "a21", 6), (2, "c", 0), (2, "b0", 5),
    (2, "a21", 7), (2, "b0", 3), (2, "a21", 8), (2, "c", 1), (2, "c", 2), (1, "c", 2),
    (1, "c", 3), (2, "b0", 4), (2, "a0", 6), (2, "a0", 7), (2, "a0", 8), (2, "c", 4),
    (2, "c", 5), (2, "c", 3), (1, "d", 1), (1, "d", 0), (2, "d", 0), (2, "c", 6),
    (2, "c", 7), (2, "c", 8), (2, "b0", 6), (2, "b0", 7), (2, "b0", 8), (2, "d", 1),
    (2, "d", 2), (2, "d", 3), (2, "d", 4), (2, "d", 5), (1, "d", 2), (1, "d", 3),
    (2, "d", 6), (2, "d", 7), (2, "d", 8), (1, "e", 0), (1, "e", 1), (2, "e", 0),
    (2, "e", 1), (2, "e", 2), (2, "e", 3), (2, "e", 4), (2, "e", 5), (1, "e", 2),
    (2, "e", 6), (2, "e", 7), (2, "e", 8), (1, "e", 3), (2, "f", 0), (2, "f", 1),
    (2, "f", 2), (1, "f", 0), (1, "f", 1), (2, "f", 4), (2, "f", 3), (2, "f", 5),
    (2, "f", 7), (1, "g", 0), (1, "g", 1), (1, "f", 2), (2, "f", 6), (2, "f", 8),
    (1, "f", 3), (2, "g", 0), (2, "g", 1), (2, "g", 2), (1, "g", 2), (1, "g", 3),
    (2, "g", 3), (2, "g", 4), (2, "g", 5), (2, "g", 7), (2, "g", 6), (2, "g", 8),
)
LOADS = ((2, 0), (2, 1), (2, 2), (2, 3), (1, 0), (1, 1), (2, 4), (2, 5), (2, 6), (2, 7), (2, 8), (1, 2), (1, 3))
FIRST_LOADS = 2
DRAIN = {"d": ("a3", "a21", "a0", "b1"), "e": ("b0", "c"), "f": ("d",), "g": ("e",)}
N_COPIES = 13 * len(PIECES_TWO) + 12 * len(PIECES_ONE)


def code(x, power):
    t = x * (2.0**power)
    t2 = t * t
    return ((t2 * t2) * t2 * (t * jnp.abs(t))).astype(jnp.bfloat16)


def decode(y, power):
    y = y.astype(jnp.float32)
    quarter = lax.rsqrt(lax.rsqrt(jnp.maximum(jnp.abs(y), 2.0**-126)))
    sign = jnp.where(y < 0, -(2.0**-power), 2.0**-power)
    return quarter * lax.rsqrt(quarter) * sign


def kernel(
    d1, d2, p1, m1, p2, m2,
    np1, nm1, cv1, np2, nm2, cv2,
    d1v, d2v, pm,
    s2a, s2b, s2c, r2a, r2b, r2c,
    s1b, s1c, r1a, r1b, r1c,
    send_sem, recv_sem, load_sem,
):
    row, col, fsdp = lax.axis_index("row"), lax.axis_index("col"), lax.axis_index("fsdp")
    xh, z = row // 4, row % 4
    y, core = col // 2, col % 2

    known = {}

    def flip4(v, mask):
        if mask == 0:
            return v
        if mask == 1:
            return v + 1 - 2 * (v % 2)
        if mask == 3:
            return 3 - v
        return 2 - v + 2 * (v % 2)

    def row_of(mask):
        if ("row", mask) not in known:
            high = 1 - xh if mask & 4 else xh
            known["row", mask] = high * 4 + flip4(z, mask & 3)
        return known["row", mask]

    def col_of(mask):
        if ("col", mask) not in known:
            low = 1 - core if mask & 1 else core
            known["col", mask] = flip4(y, mask >> 1) * 2 + low
        return known["col", mask]

    for mask in range(8):
        row_of(mask)
        col_of(mask)

    def device_two(mask):
        return (row_of(mask), col, fsdp)

    def device_one(mask):
        return (row, col_of(mask), fsdp)

    orders_two = ((1, 3, 4), (3, 4, 1), (4, 1, 3))
    orders_one = ((1, 2, 6), (1, 6, 2))

    def cols(index):
        return pl.ds(pl.multiple_of(index * WIDTH, WIDTH), WIDTH)

    barrier = pltpu.get_barrier_semaphore()
    for mask in (1, 3, 4):
        pl.semaphore_signal(barrier, inc=1, device_id=device_two(mask), device_id_type=MESH)
    for mask in (1, 2, 6):
        pl.semaphore_signal(barrier, inc=1, device_id=device_one(mask), device_id_type=MESH)

    n_sent = [0]
    sent = []

    def send(src, dst, device):
        i = n_sent[0]
        n_sent[0] += 1
        if i == 0:
            pl.semaphore_wait(barrier, 6)
        copy = pltpu.make_async_remote_copy(
            src_ref=src, dst_ref=dst, send_sem=send_sem.at[i], recv_sem=recv_sem.at[i],
            device_id=device, device_id_type=MESH,
        )
        copy.start()
        sent.append(copy)
        return copy

    def drain(copies):
        for copy in copies:
            copy.wait_send()

    loads = []

    def load(src, dst):
        copy = pltpu.make_async_copy(src, dst, load_sem.at[len(loads)])
        loads.append(copy)
        return copy

    n_started = [0]

    def start_loads(count):
        for copy in loads[n_started[0] : n_started[0] + count]:
            copy.start()
        n_started[0] = min(n_started[0] + count, len(loads))

    loaded_two, loaded_one = {}, {}
    for level, k in LOADS:
        pieces, loaded, hbm, vmem = (PIECES_TWO, loaded_two, d2, d2v) if level == 2 else (PIECES_ONE, loaded_one, d1, d1v)
        rs = pl.ds(pieces[k][1], pieces[k][2])
        loaded[k] = load(hbm.at[rs], vmem.at[rs])
    loaded_pm = [load(ref, pm.at[i]) for i, ref in enumerate((p1, m1, p2, m2))]
    start_loads(FIRST_LOADS)

    def over(r0, n, body):
        def step(i, carry):
            body(pl.ds(pl.multiple_of(r0 + i * STEP, STEP), STEP))
            return carry

        lax.fori_loop(0, n // STEP, step, 0)

    def block_mask(order, e):
        mask = 0
        for bit, m in zip((4, 2, 1), order):
            if e & bit:
                mask ^= m
        return mask

    class Level:
        def __init__(self, pieces, orders, index_of, device, dv, cv, loaded, param, out, sa, sb, sc, ra, rb, rc):
            self.pieces, self.orders, self.index_of, self.device = pieces, orders, index_of, device
            self.dv, self.cv, self.loaded = dv, cv, loaded
            self.param, self.out = param, out
            self.sa, self.sb, self.sc, self.ra, self.rb, self.rc = sa, sb, sc, ra, rb, rc
            self.got = {}

        def at(self, k):
            o, r0, n = self.pieces[k]
            return self.orders[o], r0, n, pl.ds(r0, n)

        def cols(self, order, e):
            return cols(self.index_of(block_mask(order, e)))

        def give(self, k, e, stage):
            order, r0, n, rs = self.at(k)
            part = self.cv.at[rs, self.cols(order, e)]
            bit = (4, 2, 1)[stage]
            self.got[k, "g", e ^ bit] = send(part, part, self.device(order[stage]))

        def ready(self, k):
            if k in self.loaded:
                copy = self.loaded.pop(k)
                while not any(copy is started for started in loads[: n_started[0]]):
                    start_loads(1)
                copy.wait()

        def want(self, *keys):
            for key in keys:
                if key in self.got:
                    self.got.pop(key).wait_recv()

        def second(self, k, q):
            order, r0, n, rs = self.at(k)
            self.ready(k)
            self.want(self.first_key(k, 2 + q))
            c = self.cols(order, 2 + q)
            came = self.slot(k, 2 + q)

            def body(s):
                self.sb[q, s] = code(self.dv[s, c] + self.first(self.ra[came, s]), 12)

            over(r0, n, body)
            self.got[k, "b", q] = send(self.sb.at[q, rs], self.rb.at[q, rs], self.device(order[1]))

        def step_b1(self, k):
            self.second(k, 1)

        def step_b0(self, k):
            self.second(k, 0)

        def step_c(self, k):
            order, r0, n, rs = self.at(k)
            self.want(self.first_key(k, 1), (k, "b", 1))
            c = self.cols(order, 1)

            def body(s):
                total = self.dv[s, c] + self.first(self.ra[self.slot(k, 1), s]) + decode(self.rb[1, s], 12)
                self.sc[s] = code(total, 11)

            over(r0, n, body)
            self.got[k, "c", 0] = send(self.sc.at[rs], self.rc.at[rs], self.device(order[2]))

        def step_d(self, k):
            order, r0, n, rs = self.at(k)
            self.want(self.first_key(k, 0), (k, "b", 0), (k, "c", 0))
            mine = self.cols(order, 0)
            i = self.param

            def body(s):
                total = self.dv[s, mine] + self.first(self.ra[0, s])
                grad = (total + decode(self.rb[0, s], 12) + decode(self.rc[s], 11)) * 0.125
                moment = 0.9 * pm[i + 1, s] + grad
                params = pm[i, s] - 0.7 * (grad + 0.9 * moment)
                self.out[1][s] = moment
                self.out[0][s] = params
                self.cv[s, mine] = params.astype(jnp.bfloat16)

            over(r0, n, body)
            self.give(k, 0, 2)
            self.give(k, 0, 1)
            self.give(k, 0, 0)

        def step_e(self, k):
            self.want((k, "g", 1))
            self.give(k, 1, 1)
            self.give(k, 1, 0)

        def step_f(self, k):
            self.want((k, "g", 2))
            self.give(k, 2, 0)
            self.want((k, "g", 3))
            self.give(k, 3, 0)

        def step_g(self, k):
            self.want(*((k, "g", e) for e in (4, 5, 6, 7)))

    class Two(Level):
        def first(self, x):
            return decode(x, 13)

        def slot(self, k, q):
            return q

        def first_key(self, k, q):
            return (k, "a", (0, 1, 1, 3)[q])

        def first_send(self, k, low, count):
            order, r0, n, rs = self.at(k)
            self.ready(k)
            places = [(q, self.cols(order, 4 + q)) for q in range(low, low + count)]

            def body(s):
                for q, c in places:
                    self.sa[q, s] = code(self.dv[s, c], 13)

            over(r0, n, body)
            slots = pl.ds(low, count)
            self.got[k, "a", low] = send(self.sa.at[slots, rs], self.ra.at[slots, rs], self.device(order[0]))

        def step_a3(self, k):
            self.first_send(k, 3, 1)

        def step_a21(self, k):
            self.first_send(k, 1, 2)

        def step_a0(self, k):
            self.first_send(k, 0, 1)

    class One(Level):
        def first(self, x):
            return x

        def slot(self, k, q):
            return q if k % 2 == 0 else (0, 2, 1, 3)[q]

        def first_key(self, k, q):
            return (k // 2, "a", self.slot(k, q))

        def step_a3(self, k):
            order, r0, n, rs = self.at(k)
            if k % 2:
                return
            rs = pl.ds(r0, n + self.pieces[k + 1][2])
            for q in (3, 2, 1, 0):
                part = d1.at[rs, self.cols(order, 4 + q)]
                self.got[k // 2, "a", q] = send(part, self.ra.at[q, rs], self.device(order[0]))

    two = Two(PIECES_TWO, orders_two, row_of, device_two, d2v, cv2, loaded_two, 2, (np2, nm2), s2a, s2b, s2c, r2a, r2b, r2c)
    one = One(PIECES_ONE, orders_one, col_of, device_one, d1v, cv1, loaded_one, 0, (np1, nm1), None, s1b, s1c, r1a, r1b, r1c)
    unsent = {}
    for level, step, k in PLAN:
        if step == "d" and loaded_pm:
            for copy in loaded_pm:
                copy.wait()
            loaded_pm.clear()
        getattr(two if level == 2 else one, "step_" + step)(k)
        start_loads(2)
        unsent[level, k, step] = tuple(sent)
        sent.clear()
        for early in DRAIN.get(step, ()):
            drain(unsent.pop((level, k, early), ()))
    for copies in unsent.values():
        drain(copies)
    assert n_sent[0] == N_COPIES


def write_out(*refs):
    sems = refs[12]
    copies = [pltpu.make_async_copy(refs[i], refs[6 + i], sems.at[i]) for i in range(6)]
    for copy in copies:
        copy.start()
    for copy in copies:
        copy.wait()


def body(delta_one, delta_two, params_one, moment_one, params_two, moment_two):
    args = (delta_one[0, 0], delta_two[0, 0], params_one[0], moment_one[0], params_two[0], moment_two[0])
    hbm = pl.BlockSpec(memory_space=pltpu.HBM)
    vmem = pl.BlockSpec(memory_space=pltpu.VMEM)
    small = jax.ShapeDtypeStruct((ROWS, WIDTH), jnp.float32)
    wide = jax.ShapeDtypeStruct((ROWS, 8 * WIDTH), jnp.bfloat16)
    f32, bf16 = jnp.float32, jnp.bfloat16
    n_local = len(PIECES_TWO) + len(PIECES_ONE)
    outs = pl.pallas_call(
        kernel,
        out_shape=tuple(pltpu.VMEM(x.shape, x.dtype) for x in (small, small, wide, small, small, wide)),
        in_specs=[hbm] * 6,
        out_specs=[vmem] * 6,
        scratch_shapes=[
            pltpu.VMEM((ROWS, 8 * WIDTH), f32),
            pltpu.VMEM((ROWS, 8 * WIDTH), f32),
            pltpu.VMEM((4, ROWS, WIDTH), f32),
            pltpu.VMEM((4, ROWS, WIDTH), bf16),
            pltpu.VMEM((2, ROWS, WIDTH), bf16),
            pltpu.VMEM((ROWS, WIDTH), bf16),
            pltpu.VMEM((4, ROWS, WIDTH), bf16),
            pltpu.VMEM((2, ROWS, WIDTH), bf16),
            pltpu.VMEM((ROWS, WIDTH), bf16),
            pltpu.VMEM((2, ROWS, WIDTH), bf16),
            pltpu.VMEM((ROWS, WIDTH), bf16),
            pltpu.VMEM((4, ROWS, WIDTH), f32),
            pltpu.VMEM((2, ROWS, WIDTH), bf16),
            pltpu.VMEM((ROWS, WIDTH), bf16),
            pltpu.SemaphoreType.DMA((N_COPIES,)),
            pltpu.SemaphoreType.DMA((N_COPIES,)),
            pltpu.SemaphoreType.DMA((n_local + 4,)),
        ],
        compiler_params=pltpu.CompilerParams(
            collective_id=0, has_side_effects=True, vmem_limit_bytes=32 * 1024 * 1024
        ),
        name="outer_step",
    )(*(pltpu.with_memory_space_constraint(x, pltpu.HBM) for x in args))
    outs = pl.pallas_call(
        write_out,
        out_shape=(small, small, wide, small, small, wide),
        in_specs=[vmem] * 6,
        out_specs=[hbm] * 6,
        scratch_shapes=[pltpu.SemaphoreType.DMA((6,))],
        compiler_params=pltpu.CompilerParams(vmem_limit_bytes=1024 * 1024),
        name="write_out",
    )(*(pltpu.with_memory_space_constraint(x, pltpu.VMEM) for x in outs))
    return tuple(out[None] for out in outs)


def solution(mesh):
    placed = (
        P("row", "col", "fsdp", None),
        P("row", "col", "fsdp", None),
        P("row", "fsdp", "col"),
        P("row", "fsdp", "col"),
        P("col", "fsdp", "row"),
        P("col", "fsdp", "row"),
    )
    return jax.shard_map(
        body,
        mesh=mesh,
        in_specs=placed,
        out_specs=(
            P("row", "fsdp", "col"),
            P("row", "fsdp", "col"),
            P("row", "fsdp", None),
            P("col", "fsdp", "row"),
            P("col", "fsdp", "row"),
            P("col", "fsdp", None),
        ),
        check_vma=False,
    )
```

```python
import jax
import jax.numpy as jnp
from jax import lax
from jax.experimental import pallas as pl
from jax.experimental.pallas import tpu as pltpu
from jax.sharding import PartitionSpec as P

MESH = pl.DeviceIdType.MESH
ROWS, WIDTH = 512, 256
STEP = 16
PIECES_TWO = ((0, 0, 80), (1, 80, 80), (2, 160, 64), (0, 224, 96), (1, 320, 96), (2, 416, 96))
PIECES_ONE = ((0, 0, 176), (0, 176, 176), (0, 352, 160))
PLAN = (
    (2, "a3", 0), (2, "a21", 0), (1, "a3", 0), (2, "a3", 1), (2, "a21", 1), (1, "a3", 1),
    (2, "a3", 2), (2, "a21", 2), (1, "a3", 2), (2, "a3", 3), (2, "a3", 4), (2, "a3", 5),
    (2, "b1", 0), (2, "a21", 3), (1, "b1", 0), (2, "b1", 1), (2, "b1", 2), (2, "a21", 4),
    (2, "a21", 5), (2, "b0", 0), (2, "b0", 1), (1, "b1", 1), (2, "b1", 3), (2, "b1", 4),
    (2, "b1", 5), (2, "b0", 2), (2, "c", 0), (2, "c", 1), (1, "b1", 2), (2, "c", 2),
    (2, "b0", 3), (2, "a0", 0), (2, "b0", 4), (2, "b0", 5), (2, "a0", 1), (2, "c", 5),
    (2, "a0", 2), (2, "a0", 3), (1, "d", 0), (2, "c", 3), (2, "c", 4), (2, "a0", 4),
    (2, "d", 0), (2, "a0", 5), (2, "d", 1), (1, "d", 1), (2, "d", 2), (2, "d", 3),
    (2, "d", 4), (2, "d", 5), (1, "d", 2), (2, "e", 0), (2, "e", 1), (2, "e", 2),
    (2, "e", 3), (2, "e", 4), (1, "e", 0), (2, "e", 5), (2, "f", 0), (2, "f", 1),
    (2, "f", 2), (2, "f", 3), (2, "f", 4), (1, "g", 0), (2, "f", 5), (1, "e", 1),
    (2, "g", 0), (2, "g", 1), (2, "g", 2), (1, "e", 2), (1, "g", 1), (2, "g", 3),
    (2, "g", 4), (2, "g", 5), (1, "g", 2),
)
ORDERS = ((1, 3, 4), (3, 4, 1), (4, 1, 3))
LOADS = ((2, 0), (2, 1), (2, 2), (2, 3), (2, 4), (2, 5), (1, 0), (1, 1), (1, 2))
FIRST_LOADS = 2
KINDS = 4
ARRIVALS = 7 * len(PIECES_TWO) + 4 * len(PIECES_ONE)


def code(x, power):
    t = x * (2.0**power)
    t2 = t * t
    return ((t2 * t2) * t2 * (t * jnp.abs(t))).astype(jnp.bfloat16)


def decode(y, power):
    y = y.astype(jnp.float32)
    quarter = lax.rsqrt(lax.rsqrt(jnp.maximum(jnp.abs(y), 2.0**-126)))
    sign = jnp.where(y < 0, -(2.0**-power), 2.0**-power)
    return quarter * lax.rsqrt(quarter) * sign


def kernel(
    d1, d2, p1, m1, p2, m2,
    np1, nm1, cv1, np2, nm2, cv2,
    d1v, d2v, pm,
    s2a, s2b, s2c, r2a, r2b, r2c,
    s1b, r1a, r1b,
    send_sem, recv_sem, load_sem,
):
    row, col, fsdp = lax.axis_index("row"), lax.axis_index("col"), lax.axis_index("fsdp")
    xh, z = row // 4, row % 4
    y, core = col // 2, col % 2

    known = {}

    def flip4(v, mask):
        if mask == 0:
            return v
        if mask == 1:
            return v + 1 - 2 * (v % 2)
        if mask == 3:
            return 3 - v
        return 2 - v + 2 * (v % 2)

    def row_of(mask):
        if ("row", mask) not in known:
            high = 1 - xh if mask & 4 else xh
            known["row", mask] = high * 4 + flip4(z, mask & 3)
        return known["row", mask]

    def col_of(mask):
        if ("col", mask) not in known:
            low = 1 - core if mask & 1 else core
            known["col", mask] = flip4(y, mask >> 1) * 2 + low
        return known["col", mask]

    for mask in range(8):
        row_of(mask)
        col_of(mask)

    def device_two(mask):
        return (row_of(mask), col, fsdp)

    def device_one(mask):
        return (row, col_of(mask), fsdp)

    def cols(index):
        return pl.ds(pl.multiple_of(index * WIDTH, WIDTH), WIDTH)

    barrier = pltpu.get_barrier_semaphore()
    for mask in (1, 3, 4):
        pl.semaphore_signal(barrier, inc=1, device_id=device_two(mask), device_id_type=MESH)
    for mask in (1, 2, 4, 6):
        pl.semaphore_signal(barrier, inc=1, device_id=device_one(mask), device_id_type=MESH)

    def block_mask(order, e):
        mask = 0
        for bit, m in zip((4, 2, 1), order):
            if e & bit:
                mask ^= m
        return mask

    arrivals = {}

    def arrival(key):
        return recv_sem.at[arrivals.setdefault(key, len(arrivals))]

    def send(src, dst, device, kind, key):
        if not arrivals:
            pl.semaphore_wait(barrier, 7)
        pltpu.make_async_remote_copy(
            src_ref=src, dst_ref=dst, send_sem=send_sem.at[kind], recv_sem=arrival(key),
            device_id=device, device_id_type=MESH,
        ).start()

    def wait_bytes(sem, ref):
        pltpu.make_async_copy(ref, ref, sem).wait()

    loads = []

    def load(src, dst):
        copy = pltpu.make_async_copy(src, dst, load_sem.at[len(loads)])
        loads.append(copy)
        return copy

    n_started = [0]

    def start_loads(count):
        for copy in loads[n_started[0] : n_started[0] + count]:
            copy.start()
        n_started[0] = min(n_started[0] + count, len(loads))

    loaded_two, loaded_one = {}, {}
    for level, k in LOADS:
        pieces, loaded, hbm, vmem = (PIECES_TWO, loaded_two, d2, d2v) if level == 2 else (PIECES_ONE, loaded_one, d1, d1v)
        rs = pl.ds(pieces[k][1], pieces[k][2])
        loaded[k] = load(hbm.at[rs], vmem.at[rs])
    n_rows = len(loads)
    for i, ref in enumerate((p1, m1, p2, m2)):
        loads.append(pltpu.make_async_copy(ref, pm.at[i], load_sem.at[n_rows]))
    start_loads(FIRST_LOADS)

    def over(r0, n, body):
        def step(i, carry):
            body(pl.ds(pl.multiple_of(r0 + i * STEP, STEP), STEP))
            return carry

        lax.fori_loop(0, n // STEP, step, 0)

    class Level:
        def __init__(self, pieces, index_of, device, dv, cv, loaded, param, out, buffers):
            self.pieces, self.index_of, self.device = pieces, index_of, device
            self.dv, self.cv, self.loaded = dv, cv, loaded
            self.param, self.out = param, out
            self.sa, self.sb, self.sc, self.ra, self.rb, self.rc = buffers
            self.waited = set()

        def rows(self, k):
            r0, n = self.pieces[k][1:]
            return r0, n, pl.ds(r0, n)

        def cols(self, mask):
            return cols(self.index_of(mask))

        def ready(self, k):
            if k in self.loaded:
                copy = self.loaded.pop(k)
                while not any(copy is started for started in loads[: n_started[0]]):
                    start_loads(1)
                copy.wait()

        def want(self, k, name, ref):
            key = (self.param, k, name)
            if key not in self.waited:
                self.waited.add(key)
                wait_bytes(arrival(key), ref)

        def want_blocks(self, k, name, count):
            self.want(k, name, self.cv.at[self.rows(k)[2], pl.ds(0, count * WIDTH)])

        def put(self, k, src, dst, link, kind, name):
            send(src, dst, self.device(link), kind + KINDS * (self.param // 2), (self.param, k, name))

        def give(self, k, mask, link, name):
            part = self.cv.at[self.rows(k)[2], self.cols(mask)]
            self.put(k, part, part, link, 3, name)

        def finish(self, k, total_of):
            r0, n, rs = self.rows(k)
            mine = self.cols(0)
            i = self.param

            def body(s):
                grad = (self.dv[s, mine] + total_of(s)) * 0.125
                moment = 0.9 * pm[i + 1, s] + grad
                params = pm[i, s] - 0.7 * (grad + 0.9 * moment)
                self.out[1][s] = moment
                self.out[0][s] = params
                self.cv[s, mine] = params.astype(jnp.bfloat16)

            over(r0, n, body)

    class Two(Level):
        def masks(self, k):
            return ORDERS[self.pieces[k][0]]

        def block(self, k, e):
            return block_mask(self.masks(k), e)

        def first_send(self, k, low, count, name):
            r0, n, rs = self.rows(k)
            self.ready(k)
            places = [(q, self.cols(self.block(k, 4 + q))) for q in range(low, low + count)]

            def body(s):
                for q, c in places:
                    self.sa[q, s] = code(self.dv[s, c], 13)

            over(r0, n, body)
            slots = pl.ds(low, count)
            self.put(k, self.sa.at[slots, rs], self.ra.at[slots, rs], self.masks(k)[0], 0, name)

        def step_a3(self, k):
            self.first_send(k, 3, 1, "a3")

        def step_a21(self, k):
            self.first_send(k, 1, 2, "a21")

        def step_a0(self, k):
            self.first_send(k, 0, 1, "last")

        def want_21(self, k):
            self.want(k, "a21", self.ra.at[pl.ds(1, 2), self.rows(k)[2]])

        def second(self, k, q, name):
            r0, n, rs = self.rows(k)
            c = self.cols(self.block(k, 2 + q))

            def body(s):
                self.sb[q, s] = code(self.dv[s, c] + decode(self.ra[2 + q, s], 13), 12)

            over(r0, n, body)
            self.put(k, self.sb.at[q, rs], self.rb.at[q, rs], self.masks(k)[1], 1, name)

        def step_b1(self, k):
            self.want(k, "a3", self.ra.at[3, self.rows(k)[2]])
            self.second(k, 1, "b1")

        def step_b0(self, k):
            self.want_21(k)
            self.second(k, 0, "last")

        def step_c(self, k):
            r0, n, rs = self.rows(k)
            self.want_21(k)
            self.want(k, "b1", self.rb.at[1, rs])
            c = self.cols(self.block(k, 1))

            def body(s):
                self.sc[s] = code(self.dv[s, c] + decode(self.ra[1, s], 13) + decode(self.rb[1, s], 12), 11)

            over(r0, n, body)
            self.put(k, self.sc.at[rs], self.rc.at[rs], self.masks(k)[2], 2, "last")

        def step_d(self, k):
            self.want_blocks(k, "last", 3)
            self.finish(k, lambda s: decode(self.ra[0, s], 13) + decode(self.rb[0, s], 12) + decode(self.rc[s], 11))
            one, two, three = self.masks(k)
            self.give(k, 0, three, "e")
            self.give(k, 0, two, "e")
            self.give(k, 0, one, "g")

        def step_e(self, k):
            one, two, three = self.masks(k)
            self.want_blocks(k, "e", 2)
            self.give(k, three, two, "f")
            self.give(k, three, one, "g")
            self.give(k, two, one, "g")

        def step_f(self, k):
            one, two, three = self.masks(k)
            self.want_blocks(k, "f", 1)
            self.give(k, two ^ three, one, "g")

        def step_g(self, k):
            self.want_blocks(k, "g", 4)

    class One(Level):
        def step_a3(self, k):
            rs = self.rows(k)[2]
            for chip in (2, 1, 3, 0):
                part = d1.at[rs, self.cols(2 * chip + 1)]
                self.put(k, part, self.ra.at[chip, rs], 1, 0, "last" if chip == 0 else "a")

        def step_b1(self, k):
            r0, n, rs = self.rows(k)
            self.ready(k)
            self.want(k, "a", self.ra.at[pl.ds(1, 3), rs])
            places = [(chip, self.cols(2 * chip)) for chip in (2, 1, 3)]

            def body(s):
                for chip, c in places:
                    self.sb[chip - 1, s] = code(self.dv[s, c] + self.ra[chip, s], 12)

            over(r0, n, body)
            for chip in (2, 1, 3):
                slot = chip - 1
                self.put(k, self.sb.at[slot, rs], self.rb.at[slot, rs], 2 * chip, 1, "last")

        def step_d(self, k):
            self.want_blocks(k, "last", 5)
            self.finish(k, lambda s: self.ra[0, s] + sum(decode(self.rb[slot, s], 12) for slot in range(3)))
            for chip in (2, 1, 3):
                self.give(k, 0, 2 * chip, "e")
            self.give(k, 0, 1, "g")

        def step_e(self, k):
            self.want_blocks(k, "e", 3)
            for chip in (1, 3, 2):
                self.give(k, 2 * chip, 1, "g")

        def step_g(self, k):
            self.want_blocks(k, "g", 4)

    two = Two(PIECES_TWO, row_of, device_two, d2v, cv2, loaded_two, 2, (np2, nm2), (s2a, s2b, s2c, r2a, r2b, r2c))
    one = One(PIECES_ONE, col_of, device_one, d1v, cv1, loaded_one, 0, (np1, nm1), (None, s1b, None, r1a, r1b, None))
    loaded_pm = False
    for level, step, k in PLAN:
        if step == "d" and not loaded_pm:
            start_loads(4)
            wait_bytes(load_sem.at[n_rows], pm)
            loaded_pm = True
        getattr(two if level == 2 else one, "step_" + step)(k)
        start_loads(2)
    gathered = pl.ds(0, 7 * WIDTH)
    sources = (r1a, s1b, None, cv1.at[:, gathered], s2a, s2b, s2c, cv2.at[:, gathered])
    for kind, source in enumerate(sources):
        if source is not None:
            wait_bytes(send_sem.at[kind], source)
    assert len(arrivals) == ARRIVALS


def write_out(*refs):
    sems = refs[12]
    copies = [pltpu.make_async_copy(refs[i], refs[6 + i], sems.at[i]) for i in range(6)]
    for copy in copies:
        copy.start()
    for copy in copies:
        copy.wait()


def body(delta_one, delta_two, params_one, moment_one, params_two, moment_two):
    args = (delta_one[0, 0], delta_two[0, 0], params_one[0], moment_one[0], params_two[0], moment_two[0])
    hbm = pl.BlockSpec(memory_space=pltpu.HBM)
    vmem = pl.BlockSpec(memory_space=pltpu.VMEM)
    small = jax.ShapeDtypeStruct((ROWS, WIDTH), jnp.float32)
    wide = jax.ShapeDtypeStruct((ROWS, 8 * WIDTH), jnp.bfloat16)
    f32, bf16 = jnp.float32, jnp.bfloat16
    n_local = len(PIECES_TWO) + len(PIECES_ONE)
    outs = pl.pallas_call(
        kernel,
        out_shape=tuple(pltpu.VMEM(x.shape, x.dtype) for x in (small, small, wide, small, small, wide)),
        in_specs=[hbm] * 6,
        out_specs=[vmem] * 6,
        scratch_shapes=[
            pltpu.VMEM((ROWS, 8 * WIDTH), f32),
            pltpu.VMEM((ROWS, 8 * WIDTH), f32),
            pltpu.VMEM((4, ROWS, WIDTH), f32),
            pltpu.VMEM((4, ROWS, WIDTH), bf16),
            pltpu.VMEM((2, ROWS, WIDTH), bf16),
            pltpu.VMEM((ROWS, WIDTH), bf16),
            pltpu.VMEM((4, ROWS, WIDTH), bf16),
            pltpu.VMEM((2, ROWS, WIDTH), bf16),
            pltpu.VMEM((ROWS, WIDTH), bf16),
            pltpu.VMEM((3, ROWS, WIDTH), bf16),
            pltpu.VMEM((4, ROWS, WIDTH), f32),
            pltpu.VMEM((3, ROWS, WIDTH), bf16),
            pltpu.SemaphoreType.DMA((2 * KINDS,)),
            pltpu.SemaphoreType.DMA((ARRIVALS,)),
            pltpu.SemaphoreType.DMA((n_local + 1,)),
        ],
        compiler_params=pltpu.CompilerParams(
            collective_id=0, has_side_effects=True, vmem_limit_bytes=32 * 1024 * 1024
        ),
        name="outer_step",
    )(*(pltpu.with_memory_space_constraint(x, pltpu.HBM) for x in args))
    outs = pl.pallas_call(
        write_out,
        out_shape=(small, small, wide, small, small, wide),
        in_specs=[vmem] * 6,
        out_specs=[hbm] * 6,
        scratch_shapes=[pltpu.SemaphoreType.DMA((6,))],
        compiler_params=pltpu.CompilerParams(vmem_limit_bytes=1024 * 1024),
        name="write_out",
    )(*(pltpu.with_memory_space_constraint(x, pltpu.VMEM) for x in outs))
    return tuple(out[None] for out in outs)


def solution(mesh):
    placed = (
        P("row", "col", "fsdp", None),
        P("row", "col", "fsdp", None),
        P("row", "fsdp", "col"),
        P("row", "fsdp", "col"),
        P("col", "fsdp", "row"),
        P("col", "fsdp", "row"),
    )
    return jax.shard_map(
        body,
        mesh=mesh,
        in_specs=placed,
        out_specs=(
            P("row", "fsdp", "col"),
            P("row", "fsdp", "col"),
            P("row", "fsdp", None),
            P("col", "fsdp", "row"),
            P("col", "fsdp", "row"),
            P("col", "fsdp", None),
        ),
        check_vma=False,
    )
```

```python
import jax
import jax.numpy as jnp
from jax import lax
from jax.experimental import pallas as pl
from jax.experimental.pallas import tpu as pltpu
from jax.sharding import PartitionSpec as P

MESH = pl.DeviceIdType.MESH
ROWS, WIDTH = 512, 256
STEP = 16
PIECES_TWO = ((0, 0, 96), (1, 96, 96), (2, 192, 80), (0, 272, 80), (1, 352, 80), (2, 432, 80))
PIECES_ONE = ((0, 0, 176), (0, 176, 176), (0, 352, 160))
PLAN = (
    (2, "a3", 0), (1, "a3", 0), (1, "a3", 1), (2, "a3", 1), (1, "a3", 2), (2, "a21", 0),
    (2, "a3", 2), (2, "a21", 1), (2, "a21", 2), (2, "a3", 3), (2, "a3", 4), (2, "a3", 5),
    (2, "a21", 3), (2, "b1", 0), (1, "b1", 0), (2, "b1", 1), (2, "a21", 4), (2, "b1", 2),
    (2, "a21", 5), (2, "a0", 0), (2, "b0", 0), (1, "b1", 1), (2, "b1", 3), (2, "b0", 1),
    (2, "b1", 4), (1, "b1", 2), (2, "b1", 5), (2, "c", 0), (2, "c", 1), (2, "c", 2),
    (2, "b0", 2), (2, "a0", 1), (2, "a0", 2), (2, "b0", 3), (2, "b0", 4), (2, "b0", 5),
    (2, "a0", 3), (2, "a0", 4), (2, "a0", 5), (1, "d", 0), (2, "c", 3), (2, "c", 4),
    (2, "c", 5), (2, "d", 0), (2, "d", 1), (1, "d", 1), (2, "d", 2), (2, "d", 4),
    (2, "d", 3), (2, "d", 5), (2, "e", 0), (1, "d", 2), (2, "e", 1), (2, "e", 2),
    (2, "e", 4), (2, "e", 3), (2, "e", 5), (1, "e", 0), (2, "f", 0), (2, "f", 1),
    (2, "f", 2), (1, "g", 0), (1, "e", 1), (2, "f", 4), (2, "f", 5), (2, "f", 3),
    (2, "g", 0), (1, "e", 2), (2, "g", 1), (2, "g", 2), (1, "g", 1), (2, "g", 4),
    (2, "g", 5), (2, "g", 3), (1, "g", 2),
)
ORDERS = ((1, 3, 4), (3, 4, 1), (4, 1, 3))
LOADS = ((2, 0), (2, 1), (2, 2), (2, 3), (2, 4), (2, 5), (1, 0), (1, 1), (1, 2))
FIRST_LOADS = 4
KINDS = 4
ARRIVALS = 7 * len(PIECES_TWO) + 4 * len(PIECES_ONE)


def code(x, power):
    t = x * (2.0**power)
    t2 = t * t
    return ((t2 * t2) * t2 * (t * jnp.abs(t))).astype(jnp.bfloat16)


def decode(y, power):
    y = y.astype(jnp.float32)
    quarter = lax.rsqrt(lax.rsqrt(jnp.maximum(jnp.abs(y), 2.0**-126)))
    sign = jnp.where(y < 0, -(2.0**-power), 2.0**-power)
    return quarter * lax.rsqrt(quarter) * sign


def kernel(
    d1, d2, p1, m1, p2, m2,
    np1, nm1, cv1, np2, nm2, cv2,
    d1v, d2v, pm,
    s2a, s2b, s2c, r2a, r2b, r2c,
    s1b, r1a, r1b,
    send_sem, recv_sem, load_sem,
):
    row, col, fsdp = lax.axis_index("row"), lax.axis_index("col"), lax.axis_index("fsdp")
    xh, z = row // 4, row % 4
    y, core = col // 2, col % 2

    known = {}

    def flip4(v, mask):
        if mask == 0:
            return v
        if mask == 1:
            return v + 1 - 2 * (v % 2)
        if mask == 3:
            return 3 - v
        return 2 - v + 2 * (v % 2)

    def row_of(mask):
        if ("row", mask) not in known:
            high = 1 - xh if mask & 4 else xh
            known["row", mask] = high * 4 + flip4(z, mask & 3)
        return known["row", mask]

    def col_of(mask):
        if ("col", mask) not in known:
            low = 1 - core if mask & 1 else core
            known["col", mask] = flip4(y, mask >> 1) * 2 + low
        return known["col", mask]

    for mask in range(8):
        row_of(mask)
        col_of(mask)

    def device_two(mask):
        return (row_of(mask), col, fsdp)

    def device_one(mask):
        return (row, col_of(mask), fsdp)

    def cols(index):
        return pl.ds(pl.multiple_of(index * WIDTH, WIDTH), WIDTH)

    barrier = pltpu.get_barrier_semaphore()
    for mask in (1, 3, 4):
        pl.semaphore_signal(barrier, inc=1, device_id=device_two(mask), device_id_type=MESH)
    for mask in (1, 2, 4, 6):
        pl.semaphore_signal(barrier, inc=1, device_id=device_one(mask), device_id_type=MESH)

    def block_mask(order, e):
        mask = 0
        for bit, m in zip((4, 2, 1), order):
            if e & bit:
                mask ^= m
        return mask

    arrivals = {}

    def arrival(key):
        return recv_sem.at[arrivals.setdefault(key, len(arrivals))]

    def send(src, dst, device, kind, key):
        if not arrivals:
            pl.semaphore_wait(barrier, 7)
        pltpu.make_async_remote_copy(
            src_ref=src, dst_ref=dst, send_sem=send_sem.at[kind], recv_sem=arrival(key),
            device_id=device, device_id_type=MESH,
        ).start()

    def wait_bytes(sem, ref):
        pltpu.make_async_copy(ref, ref, sem).wait()

    loads = []

    def load(src, dst):
        copy = pltpu.make_async_copy(src, dst, load_sem.at[len(loads)])
        loads.append(copy)
        return copy

    n_started = [0]

    def start_loads(count):
        for copy in loads[n_started[0] : n_started[0] + count]:
            copy.start()
        n_started[0] = min(n_started[0] + count, len(loads))

    loaded_two, loaded_one = {}, {}
    for level, k in LOADS:
        pieces, loaded, hbm, vmem = (PIECES_TWO, loaded_two, d2, d2v) if level == 2 else (PIECES_ONE, loaded_one, d1, d1v)
        rs = pl.ds(pieces[k][1], pieces[k][2])
        loaded[k] = load(hbm.at[rs], vmem.at[rs])
    n_rows = len(loads)
    for i, ref in enumerate((p1, m1, p2, m2)):
        loads.append(pltpu.make_async_copy(ref, pm.at[i], load_sem.at[n_rows]))
    start_loads(FIRST_LOADS)

    def over(r0, n, body):
        def step(i, carry):
            body(pl.ds(pl.multiple_of(r0 + i * STEP, STEP), STEP))
            return carry

        lax.fori_loop(0, n // STEP, step, 0)

    class Level:
        def __init__(self, pieces, index_of, device, dv, cv, loaded, param, out, buffers):
            self.pieces, self.index_of, self.device = pieces, index_of, device
            self.dv, self.cv, self.loaded = dv, cv, loaded
            self.param, self.out = param, out
            self.sa, self.sb, self.sc, self.ra, self.rb, self.rc = buffers
            self.waited = set()

        def rows(self, k):
            r0, n = self.pieces[k][1:]
            return r0, n, pl.ds(r0, n)

        def cols(self, mask):
            return cols(self.index_of(mask))

        def ready(self, k):
            if k in self.loaded:
                copy = self.loaded.pop(k)
                while not any(copy is started for started in loads[: n_started[0]]):
                    start_loads(1)
                copy.wait()

        def want(self, k, name, ref):
            key = (self.param, k, name)
            if key not in self.waited:
                self.waited.add(key)
                wait_bytes(arrival(key), ref)

        def want_blocks(self, k, name, count):
            self.want(k, name, self.cv.at[self.rows(k)[2], pl.ds(0, count * WIDTH)])

        def put(self, k, src, dst, link, kind, name):
            send(src, dst, self.device(link), kind + KINDS * (self.param // 2), (self.param, k, name))

        def give(self, k, mask, link, name):
            part = self.cv.at[self.rows(k)[2], self.cols(mask)]
            self.put(k, part, part, link, 3, name)

        def finish(self, k, total_of):
            r0, n, rs = self.rows(k)
            mine = self.cols(0)
            i = self.param

            def body(s):
                grad = (self.dv[s, mine] + total_of(s)) * 0.125
                moment = 0.9 * pm[i + 1, s] + grad
                params = pm[i, s] - 0.7 * (grad + 0.9 * moment)
                self.out[1][s] = moment
                self.out[0][s] = params
                self.cv[s, mine] = params.astype(jnp.bfloat16)

            over(r0, n, body)

    class Two(Level):
        def masks(self, k):
            return ORDERS[self.pieces[k][0]]

        def block(self, k, e):
            return block_mask(self.masks(k), e)

        def first_send(self, k, low, count, name):
            r0, n, rs = self.rows(k)
            self.ready(k)
            places = [(q, self.cols(self.block(k, 4 + q))) for q in range(low, low + count)]

            def body(s):
                for q, c in places:
                    self.sa[q, s] = code(self.dv[s, c], 13)

            over(r0, n, body)
            slots = pl.ds(low, count)
            self.put(k, self.sa.at[slots, rs], self.ra.at[slots, rs], self.masks(k)[0], 0, name)

        def step_a3(self, k):
            self.first_send(k, 3, 1, "a3")

        def step_a21(self, k):
            self.first_send(k, 1, 2, "a21")

        def step_a0(self, k):
            self.first_send(k, 0, 1, "last")

        def want_21(self, k):
            self.want(k, "a21", self.ra.at[pl.ds(1, 2), self.rows(k)[2]])

        def second(self, k, q, name):
            r0, n, rs = self.rows(k)
            c = self.cols(self.block(k, 2 + q))

            def body(s):
                self.sb[q, s] = code(self.dv[s, c] + decode(self.ra[2 + q, s], 13), 12)

            over(r0, n, body)
            self.put(k, self.sb.at[q, rs], self.rb.at[q, rs], self.masks(k)[1], 1, name)

        def step_b1(self, k):
            self.want(k, "a3", self.ra.at[3, self.rows(k)[2]])
            self.second(k, 1, "b1")

        def step_b0(self, k):
            self.want_21(k)
            self.second(k, 0, "last")

        def step_c(self, k):
            r0, n, rs = self.rows(k)
            self.want_21(k)
            self.want(k, "b1", self.rb.at[1, rs])
            c = self.cols(self.block(k, 1))

            def body(s):
                self.sc[s] = code(self.dv[s, c] + decode(self.ra[1, s], 13) + decode(self.rb[1, s], 12), 11)

            over(r0, n, body)
            self.put(k, self.sc.at[rs], self.rc.at[rs], self.masks(k)[2], 2, "last")

        def step_d(self, k):
            self.want_blocks(k, "last", 3)
            self.finish(k, lambda s: decode(self.ra[0, s], 13) + decode(self.rb[0, s], 12) + decode(self.rc[s], 11))
            one, two, three = self.masks(k)
            self.give(k, 0, three, "e")
            self.give(k, 0, two, "e")
            self.give(k, 0, one, "g")

        def step_e(self, k):
            one, two, three = self.masks(k)
            self.want_blocks(k, "e", 2)
            self.give(k, three, two, "f")
            self.give(k, three, one, "g")
            self.give(k, two, one, "g")

        def step_f(self, k):
            one, two, three = self.masks(k)
            self.want_blocks(k, "f", 1)
            self.give(k, two ^ three, one, "g")

        def step_g(self, k):
            self.want_blocks(k, "g", 4)

    class One(Level):
        def step_a3(self, k):
            rs = self.rows(k)[2]
            for chip in (2, 1, 3, 0):
                part = d1.at[rs, self.cols(2 * chip + 1)]
                self.put(k, part, self.ra.at[chip, rs], 1, 0, "last" if chip == 0 else "a")

        def step_b1(self, k):
            r0, n, rs = self.rows(k)
            self.ready(k)
            self.want(k, "a", self.ra.at[pl.ds(1, 3), rs])
            places = [(chip, self.cols(2 * chip)) for chip in (2, 1, 3)]

            def body(s):
                for chip, c in places:
                    self.sb[chip - 1, s] = code(self.dv[s, c] + self.ra[chip, s], 12)

            over(r0, n, body)
            for chip in (2, 1, 3):
                slot = chip - 1
                self.put(k, self.sb.at[slot, rs], self.rb.at[slot, rs], 2 * chip, 1, "last")

        def step_d(self, k):
            self.want_blocks(k, "last", 5)
            self.finish(k, lambda s: self.ra[0, s] + sum(decode(self.rb[slot, s], 12) for slot in range(3)))
            for chip in (2, 1, 3):
                self.give(k, 0, 2 * chip, "e")
            self.give(k, 0, 1, "g")

        def step_e(self, k):
            self.want_blocks(k, "e", 3)
            for chip in (1, 3, 2):
                self.give(k, 2 * chip, 1, "g")

        def step_g(self, k):
            self.want_blocks(k, "g", 4)

    two = Two(PIECES_TWO, row_of, device_two, d2v, cv2, loaded_two, 2, (np2, nm2), (s2a, s2b, s2c, r2a, r2b, r2c))
    one = One(PIECES_ONE, col_of, device_one, d1v, cv1, loaded_one, 0, (np1, nm1), (None, s1b, None, r1a, r1b, None))
    loaded_pm = False
    for level, step, k in PLAN:
        if step == "d" and not loaded_pm:
            start_loads(4)
            wait_bytes(load_sem.at[n_rows], pm)
            loaded_pm = True
        getattr(two if level == 2 else one, "step_" + step)(k)
        start_loads(2)
    gathered = pl.ds(0, 7 * WIDTH)
    sources = (r1a, s1b, None, cv1.at[:, gathered], s2a, s2b, s2c, cv2.at[:, gathered])
    for kind, source in enumerate(sources):
        if source is not None:
            wait_bytes(send_sem.at[kind], source)
    assert len(arrivals) == ARRIVALS


def write_out(*refs):
    sems = refs[12]
    copies = [pltpu.make_async_copy(refs[i], refs[6 + i], sems.at[i]) for i in range(6)]
    for copy in copies:
        copy.start()
    for copy in copies:
        copy.wait()


def body(delta_one, delta_two, params_one, moment_one, params_two, moment_two):
    args = (delta_one[0, 0], delta_two[0, 0], params_one[0], moment_one[0], params_two[0], moment_two[0])
    hbm = pl.BlockSpec(memory_space=pltpu.HBM)
    vmem = pl.BlockSpec(memory_space=pltpu.VMEM)
    small = jax.ShapeDtypeStruct((ROWS, WIDTH), jnp.float32)
    wide = jax.ShapeDtypeStruct((ROWS, 8 * WIDTH), jnp.bfloat16)
    f32, bf16 = jnp.float32, jnp.bfloat16
    n_local = len(PIECES_TWO) + len(PIECES_ONE)
    outs = pl.pallas_call(
        kernel,
        out_shape=tuple(pltpu.VMEM(x.shape, x.dtype) for x in (small, small, wide, small, small, wide)),
        in_specs=[hbm] * 6,
        out_specs=[vmem] * 6,
        scratch_shapes=[
            pltpu.VMEM((ROWS, 8 * WIDTH), f32),
            pltpu.VMEM((ROWS, 8 * WIDTH), f32),
            pltpu.VMEM((4, ROWS, WIDTH), f32),
            pltpu.VMEM((4, ROWS, WIDTH), bf16),
            pltpu.VMEM((2, ROWS, WIDTH), bf16),
            pltpu.VMEM((ROWS, WIDTH), bf16),
            pltpu.VMEM((4, ROWS, WIDTH), bf16),
            pltpu.VMEM((2, ROWS, WIDTH), bf16),
            pltpu.VMEM((ROWS, WIDTH), bf16),
            pltpu.VMEM((3, ROWS, WIDTH), bf16),
            pltpu.VMEM((4, ROWS, WIDTH), f32),
            pltpu.VMEM((3, ROWS, WIDTH), bf16),
            pltpu.SemaphoreType.DMA((2 * KINDS,)),
            pltpu.SemaphoreType.DMA((ARRIVALS,)),
            pltpu.SemaphoreType.DMA((n_local + 1,)),
        ],
        compiler_params=pltpu.CompilerParams(
            collective_id=0, has_side_effects=True, vmem_limit_bytes=32 * 1024 * 1024
        ),
        name="outer_step",
    )(*(pltpu.with_memory_space_constraint(x, pltpu.HBM) for x in args))
    outs = pl.pallas_call(
        write_out,
        out_shape=(small, small, wide, small, small, wide),
        in_specs=[vmem] * 6,
        out_specs=[hbm] * 6,
        scratch_shapes=[pltpu.SemaphoreType.DMA((6,))],
        compiler_params=pltpu.CompilerParams(vmem_limit_bytes=1024 * 1024),
        name="write_out",
    )(*(pltpu.with_memory_space_constraint(x, pltpu.VMEM) for x in outs))
    return tuple(out[None] for out in outs)


def solution(mesh):
    placed = (
        P("row", "col", "fsdp", None),
        P("row", "col", "fsdp", None),
        P("row", "fsdp", "col"),
        P("row", "fsdp", "col"),
        P("col", "fsdp", "row"),
        P("col", "fsdp", "row"),
    )
    return jax.shard_map(
        body,
        mesh=mesh,
        in_specs=placed,
        out_specs=(
            P("row", "fsdp", "col"),
            P("row", "fsdp", "col"),
            P("row", "fsdp", None),
            P("col", "fsdp", "row"),
            P("col", "fsdp", "row"),
            P("col", "fsdp", None),
        ),
        check_vma=False,
    )
```

```python
import jax
import jax.numpy as jnp
from jax import lax
from jax.experimental import pallas as pl
from jax.experimental.pallas import tpu as pltpu
from jax.sharding import PartitionSpec as P

MESH = pl.DeviceIdType.MESH
ROWS, WIDTH = 512, 256
STEP = 16
PIECES_TWO = ((0, 0, 96), (1, 96, 96), (2, 192, 80), (0, 272, 80), (1, 352, 80), (2, 432, 80))
PIECES_ONE = ((0, 0, 160), (0, 160, 160), (0, 320, 192))
PLAN = (
    (2, "a3", 0), (1, "a3", 0), (1, "a3", 1), (2, "a3", 1), (1, "a3", 2), (2, "a3", 2),
    (2, "a21", 0), (2, "a21", 1), (2, "a21", 2), (2, "a3", 3), (2, "a3", 4), (2, "a3", 5),
    (2, "a21", 3), (2, "b1", 0), (1, "b1", 0), (2, "b1", 1), (2, "a21", 4), (2, "b1", 2),
    (2, "a21", 5), (1, "b1", 1), (2, "b0", 0), (2, "b0", 1), (2, "b0", 2), (2, "b1", 3),
    (2, "b1", 4), (2, "b1", 5), (1, "b1", 2), (2, "c", 0), (2, "c", 1), (2, "b0", 3),
    (2, "a0", 0), (2, "a0", 1), (2, "a0", 2), (2, "a0", 3), (2, "c", 2), (2, "b0", 4),
    (2, "b0", 5), (2, "a0", 4), (1, "d", 0), (2, "c", 5), (2, "c", 3), (2, "c", 4),
    (2, "a0", 5), (2, "d", 0), (1, "d", 1), (2, "d", 1), (2, "d", 2), (2, "d", 3),
    (2, "d", 4), (2, "d", 5), (2, "e", 0), (1, "d", 2), (2, "e", 1), (2, "e", 2),
    (2, "e", 3), (2, "e", 4), (1, "e", 0), (2, "e", 5), (2, "f", 0), (2, "f", 1),
    (1, "e", 1), (2, "f", 2), (1, "g", 0), (2, "f", 4), (2, "f", 3), (2, "f", 5),
    (1, "g", 1), (2, "g", 0), (1, "e", 2), (2, "g", 1), (2, "g", 2), (2, "g", 3),
    (2, "g", 4), (2, "g", 5), (1, "g", 2),
)
ORDERS = ((1, 3, 4), (3, 4, 1), (4, 1, 3))
LOADS = ((2, 0), (2, 1), (2, 2), (2, 3), (2, 4), (2, 5), (1, 0), (1, 1), (1, 2))
FIRST_LOADS = 4
KINDS = 4
ARRIVALS = 7 * len(PIECES_TWO) + 4 * len(PIECES_ONE)


def code(x, power):
    t = x * (2.0**power)
    t2 = t * t
    return ((t2 * t2) * t2 * (t * jnp.abs(t))).astype(jnp.bfloat16)


def decode(y, power):
    y = y.astype(jnp.float32)
    quarter = lax.rsqrt(lax.rsqrt(jnp.maximum(jnp.abs(y), 2.0**-126)))
    sign = jnp.where(y < 0, -(2.0**-power), 2.0**-power)
    return quarter * lax.rsqrt(quarter) * sign


def kernel(
    d1, d2, p1, m1, p2, m2,
    np1, nm1, cv1, np2, nm2, cv2,
    d1v, d2v, pm,
    s2a, s2b, s2c, r2a, r2b, r2c,
    s1b, r1a, r1b,
    send_sem, recv_sem, load_sem,
):
    row, col, fsdp = lax.axis_index("row"), lax.axis_index("col"), lax.axis_index("fsdp")
    xh, z = row // 4, row % 4
    y, core = col // 2, col % 2

    known = {}

    def flip4(v, mask):
        if mask == 0:
            return v
        if mask == 1:
            return v + 1 - 2 * (v % 2)
        if mask == 3:
            return 3 - v
        return 2 - v + 2 * (v % 2)

    def row_of(mask):
        if ("row", mask) not in known:
            high = 1 - xh if mask & 4 else xh
            known["row", mask] = high * 4 + flip4(z, mask & 3)
        return known["row", mask]

    def col_of(mask):
        if ("col", mask) not in known:
            low = 1 - core if mask & 1 else core
            known["col", mask] = flip4(y, mask >> 1) * 2 + low
        return known["col", mask]

    for mask in range(8):
        row_of(mask)
        col_of(mask)

    def device_two(mask):
        return (row_of(mask), col, fsdp)

    def device_one(mask):
        return (row, col_of(mask), fsdp)

    def cols(index):
        return pl.ds(pl.multiple_of(index * WIDTH, WIDTH), WIDTH)

    barrier = pltpu.get_barrier_semaphore()
    for mask in (1, 3, 4):
        pl.semaphore_signal(barrier, inc=1, device_id=device_two(mask), device_id_type=MESH)
    for mask in (1, 2, 4, 6):
        pl.semaphore_signal(barrier, inc=1, device_id=device_one(mask), device_id_type=MESH)

    def block_mask(order, e):
        mask = 0
        for bit, m in zip((4, 2, 1), order):
            if e & bit:
                mask ^= m
        return mask

    arrivals = {}

    def arrival(key):
        return recv_sem.at[arrivals.setdefault(key, len(arrivals))]

    def send(src, dst, device, kind, key):
        if not arrivals:
            pl.semaphore_wait(barrier, 7)
        pltpu.make_async_remote_copy(
            src_ref=src, dst_ref=dst, send_sem=send_sem.at[kind], recv_sem=arrival(key),
            device_id=device, device_id_type=MESH,
        ).start()

    def wait_bytes(sem, ref):
        pltpu.make_async_copy(ref, ref, sem).wait()

    loads = []

    def load(src, dst):
        copy = pltpu.make_async_copy(src, dst, load_sem.at[len(loads)])
        loads.append(copy)
        return copy

    n_started = [0]

    def start_loads(count):
        for copy in loads[n_started[0] : n_started[0] + count]:
            copy.start()
        n_started[0] = min(n_started[0] + count, len(loads))

    loaded_two, loaded_one = {}, {}
    for level, k in LOADS:
        pieces, loaded, hbm, vmem = (PIECES_TWO, loaded_two, d2, d2v) if level == 2 else (PIECES_ONE, loaded_one, d1, d1v)
        rs = pl.ds(pieces[k][1], pieces[k][2])
        loaded[k] = load(hbm.at[rs], vmem.at[rs])
    n_rows = len(loads)
    for i, ref in enumerate((p1, m1, p2, m2)):
        loads.append(pltpu.make_async_copy(ref, pm.at[i], load_sem.at[n_rows]))
    start_loads(FIRST_LOADS)

    def over(r0, n, body):
        def step(i, carry):
            body(pl.ds(pl.multiple_of(r0 + i * STEP, STEP), STEP))
            return carry

        lax.fori_loop(0, n // STEP, step, 0)

    class Level:
        def __init__(self, pieces, index_of, device, dv, cv, loaded, param, out, buffers):
            self.pieces, self.index_of, self.device = pieces, index_of, device
            self.dv, self.cv, self.loaded = dv, cv, loaded
            self.param, self.out = param, out
            self.sa, self.sb, self.sc, self.ra, self.rb, self.rc = buffers
            self.waited = set()

        def rows(self, k):
            r0, n = self.pieces[k][1:]
            return r0, n, pl.ds(r0, n)

        def cols(self, mask):
            return cols(self.index_of(mask))

        def ready(self, k):
            if k in self.loaded:
                copy = self.loaded.pop(k)
                while not any(copy is started for started in loads[: n_started[0]]):
                    start_loads(1)
                copy.wait()

        def want(self, k, name, ref):
            key = (self.param, k, name)
            if key not in self.waited:
                self.waited.add(key)
                wait_bytes(arrival(key), ref)

        def want_blocks(self, k, name, count):
            self.want(k, name, self.cv.at[self.rows(k)[2], pl.ds(0, count * WIDTH)])

        def put(self, k, src, dst, link, kind, name):
            send(src, dst, self.device(link), kind + KINDS * (self.param // 2), (self.param, k, name))

        def give(self, k, mask, link, name):
            part = self.cv.at[self.rows(k)[2], self.cols(mask)]
            self.put(k, part, part, link, 3, name)

        def finish(self, k, total_of):
            r0, n, rs = self.rows(k)
            mine = self.cols(0)
            i = self.param

            def body(s):
                grad = (self.dv[s, mine] + total_of(s)) * 0.125
                moment = 0.9 * pm[i + 1, s] + grad
                params = pm[i, s] - 0.7 * (grad + 0.9 * moment)
                self.out[1][s] = moment
                self.out[0][s] = params
                self.cv[s, mine] = params.astype(jnp.bfloat16)

            over(r0, n, body)

    class Two(Level):
        def masks(self, k):
            return ORDERS[self.pieces[k][0]]

        def block(self, k, e):
            return block_mask(self.masks(k), e)

        def first_send(self, k, low, count, name):
            r0, n, rs = self.rows(k)
            self.ready(k)
            places = [(q, self.cols(self.block(k, 4 + q))) for q in range(low, low + count)]

            def body(s):
                for q, c in places:
                    self.sa[q, s] = code(self.dv[s, c], 13)

            over(r0, n, body)
            slots = pl.ds(low, count)
            self.put(k, self.sa.at[slots, rs], self.ra.at[slots, rs], self.masks(k)[0], 0, name)

        def step_a3(self, k):
            self.first_send(k, 3, 1, "a3")

        def step_a21(self, k):
            self.first_send(k, 1, 2, "a21")

        def step_a0(self, k):
            self.first_send(k, 0, 1, "last")

        def want_21(self, k):
            self.want(k, "a21", self.ra.at[pl.ds(1, 2), self.rows(k)[2]])

        def second(self, k, q, name):
            r0, n, rs = self.rows(k)
            c = self.cols(self.block(k, 2 + q))

            def body(s):
                self.sb[q, s] = code(self.dv[s, c] + decode(self.ra[2 + q, s], 13), 12)

            over(r0, n, body)
            self.put(k, self.sb.at[q, rs], self.rb.at[q, rs], self.masks(k)[1], 1, name)

        def step_b1(self, k):
            self.want(k, "a3", self.ra.at[3, self.rows(k)[2]])
            self.second(k, 1, "b1")

        def step_b0(self, k):
            self.want_21(k)
            self.second(k, 0, "last")

        def step_c(self, k):
            r0, n, rs = self.rows(k)
            self.want_21(k)
            self.want(k, "b1", self.rb.at[1, rs])
            c = self.cols(self.block(k, 1))

            def body(s):
                self.sc[s] = code(self.dv[s, c] + decode(self.ra[1, s], 13) + decode(self.rb[1, s], 12), 11)

            over(r0, n, body)
            self.put(k, self.sc.at[rs], self.rc.at[rs], self.masks(k)[2], 2, "last")

        def step_d(self, k):
            self.want_blocks(k, "last", 3)
            self.finish(k, lambda s: decode(self.ra[0, s], 13) + decode(self.rb[0, s], 12) + decode(self.rc[s], 11))
            one, two, three = self.masks(k)
            self.give(k, 0, three, "e")
            self.give(k, 0, two, "e")
            self.give(k, 0, one, "g")

        def step_e(self, k):
            one, two, three = self.masks(k)
            self.want_blocks(k, "e", 2)
            self.give(k, three, two, "f")
            self.give(k, three, one, "g")
            self.give(k, two, one, "g")

        def step_f(self, k):
            one, two, three = self.masks(k)
            self.want_blocks(k, "f", 1)
            self.give(k, two ^ three, one, "g")

        def step_g(self, k):
            self.want_blocks(k, "g", 4)

    class One(Level):
        def step_a3(self, k):
            rs = self.rows(k)[2]
            for chip in (2, 1, 3, 0):
                part = d1.at[rs, self.cols(2 * chip + 1)]
                self.put(k, part, self.ra.at[chip, rs], 1, 0, "last" if chip == 0 else "a")

        def step_b1(self, k):
            r0, n, rs = self.rows(k)
            self.ready(k)
            self.want(k, "a", self.ra.at[pl.ds(1, 3), rs])
            places = [(chip, self.cols(2 * chip)) for chip in (2, 1, 3)]

            def body(s):
                for chip, c in places:
                    self.sb[chip - 1, s] = code(self.dv[s, c] + self.ra[chip, s], 12)

            over(r0, n, body)
            for chip in (2, 1, 3):
                slot = chip - 1
                self.put(k, self.sb.at[slot, rs], self.rb.at[slot, rs], 2 * chip, 1, "last")

        def step_d(self, k):
            self.want_blocks(k, "last", 5)
            self.finish(k, lambda s: self.ra[0, s] + sum(decode(self.rb[slot, s], 12) for slot in range(3)))
            for chip in (2, 1, 3):
                self.give(k, 0, 2 * chip, "e")
            self.give(k, 0, 1, "g")

        def step_e(self, k):
            self.want_blocks(k, "e", 3)
            for chip in (1, 3, 2):
                self.give(k, 2 * chip, 1, "g")

        def step_g(self, k):
            self.want_blocks(k, "g", 4)

    two = Two(PIECES_TWO, row_of, device_two, d2v, cv2, loaded_two, 2, (np2, nm2), (s2a, s2b, s2c, r2a, r2b, r2c))
    one = One(PIECES_ONE, col_of, device_one, d1v, cv1, loaded_one, 0, (np1, nm1), (None, s1b, None, r1a, r1b, None))
    loaded_pm = False
    for level, step, k in PLAN:
        if step == "d" and not loaded_pm:
            start_loads(4)
            wait_bytes(load_sem.at[n_rows], pm)
            loaded_pm = True
        getattr(two if level == 2 else one, "step_" + step)(k)
        start_loads(2)
    gathered = pl.ds(0, 7 * WIDTH)
    sources = (r1a, s1b, None, cv1.at[:, gathered], s2a, s2b, s2c, cv2.at[:, gathered])
    for kind, source in enumerate(sources):
        if source is not None:
            wait_bytes(send_sem.at[kind], source)
    assert len(arrivals) == ARRIVALS


def write_out(*refs):
    sems = refs[12]
    copies = [pltpu.make_async_copy(refs[i], refs[6 + i], sems.at[i]) for i in range(6)]
    for copy in copies:
        copy.start()
    for copy in copies:
        copy.wait()


def body(delta_one, delta_two, params_one, moment_one, params_two, moment_two):
    args = (delta_one[0, 0], delta_two[0, 0], params_one[0], moment_one[0], params_two[0], moment_two[0])
    hbm = pl.BlockSpec(memory_space=pltpu.HBM)
    vmem = pl.BlockSpec(memory_space=pltpu.VMEM)
    small = jax.ShapeDtypeStruct((ROWS, WIDTH), jnp.float32)
    wide = jax.ShapeDtypeStruct((ROWS, 8 * WIDTH), jnp.bfloat16)
    f32, bf16 = jnp.float32, jnp.bfloat16
    n_local = len(PIECES_TWO) + len(PIECES_ONE)
    outs = pl.pallas_call(
        kernel,
        out_shape=tuple(pltpu.VMEM(x.shape, x.dtype) for x in (small, small, wide, small, small, wide)),
        in_specs=[hbm] * 6,
        out_specs=[vmem] * 6,
        scratch_shapes=[
            pltpu.VMEM((ROWS, 8 * WIDTH), f32),
            pltpu.VMEM((ROWS, 8 * WIDTH), f32),
            pltpu.VMEM((4, ROWS, WIDTH), f32),
            pltpu.VMEM((4, ROWS, WIDTH), bf16),
            pltpu.VMEM((2, ROWS, WIDTH), bf16),
            pltpu.VMEM((ROWS, WIDTH), bf16),
            pltpu.VMEM((4, ROWS, WIDTH), bf16),
            pltpu.VMEM((2, ROWS, WIDTH), bf16),
            pltpu.VMEM((ROWS, WIDTH), bf16),
            pltpu.VMEM((3, ROWS, WIDTH), bf16),
            pltpu.VMEM((4, ROWS, WIDTH), f32),
            pltpu.VMEM((3, ROWS, WIDTH), bf16),
            pltpu.SemaphoreType.DMA((2 * KINDS,)),
            pltpu.SemaphoreType.DMA((ARRIVALS,)),
            pltpu.SemaphoreType.DMA((n_local + 1,)),
        ],
        compiler_params=pltpu.CompilerParams(
            collective_id=0, has_side_effects=True, vmem_limit_bytes=32 * 1024 * 1024
        ),
        name="outer_step",
    )(*(pltpu.with_memory_space_constraint(x, pltpu.HBM) for x in args))
    outs = pl.pallas_call(
        write_out,
        out_shape=(small, small, wide, small, small, wide),
        in_specs=[vmem] * 6,
        out_specs=[hbm] * 6,
        scratch_shapes=[pltpu.SemaphoreType.DMA((6,))],
        compiler_params=pltpu.CompilerParams(vmem_limit_bytes=1024 * 1024),
        name="write_out",
    )(*(pltpu.with_memory_space_constraint(x, pltpu.VMEM) for x in outs))
    return tuple(out[None] for out in outs)


def solution(mesh):
    placed = (
        P("row", "col", "fsdp", None),
        P("row", "col", "fsdp", None),
        P("row", "fsdp", "col"),
        P("row", "fsdp", "col"),
        P("col", "fsdp", "row"),
        P("col", "fsdp", "row"),
    )
    return jax.shard_map(
        body,
        mesh=mesh,
        in_specs=placed,
        out_specs=(
            P("row", "fsdp", "col"),
            P("row", "fsdp", "col"),
            P("row", "fsdp", None),
            P("col", "fsdp", "row"),
            P("col", "fsdp", "row"),
            P("col", "fsdp", None),
        ),
        check_vma=False,
    )
```
